128 devices in a mesh: dp: 4 (over x), chan: 32 (over z, y, core).
Axes of the slice: x: 4, y: 4, z: 4, core: 2. Of those that a mesh axis runs over, the one named last changes fastest.
Arguments:
- loaded: bfloat16 [256, 4096, 256], P(None, ('dp', 'chan')), may hold values from -6 to 6
- pack_dest: int32 [4096], P(('dp', 'chan')), may hold values from 0 to 4095, as said below
- clip_lengths: int32 [512], replicated, may hold values from 1 to 32, 4096 in all
- weight_one: bfloat16 [12, 256, 256], P(None, 'chan'), may hold values from -0.109375 to 0.109375
- weight_two: bfloat16 [3, 256, 256], P(None, 'chan'), may hold values from -0.21875 to 0.21875
- weight_three: bfloat16 [3, 256, 256], P(None, 'chan'), may hold values from -0.21875 to 0.21875
- norm_gains: float32 [3, 256], replicated, may hold values from 0.5 to 2
- latent_grad: bfloat16 [256, 262144], P(None, ('dp', 'chan')), may hold values from -0.046875 to 0.046875
Outputs:
- latent: bfloat16 [256, 262144], P(None, ('dp', 'chan'))
- grad_one: float32 [12, 256, 256], P(None, 'chan')
- grad_two: float32 [3, 256, 256], P(None, 'chan')
- grad_three: float32 [3, 256, 256], P(None, 'chan')
- gain_grad: float32 [3, 256], replicated
The draws below stay inside these ranges and needn't reach their ends.
Inputs may be any that keep to these rules, and one draw needn't show every extreme that they name: `pack_dest`: a permutation of the packed positions: with b = i * 32 + s the index of a device (i its dp index, s its chan index), the frames loaded at rows b * 32 to (b + 1) * 32 - 1 go exactly 1 to each device e = i * 32 + r of the same dp index, to the positions e * 32 + s + k, k < 1. `clip_lengths`: clip lengths in packed frames, summing to 4096.
All inputs are finite; a program needn't handle non-finite values.
Results may differ from the reference program's by a relative error of at most 0.008.
Values may be sent and summed in bfloat16 or wider, within the bound.
A program may use at most 128 MiB of HBM per device.

```python
import math
import jax
import jax.numpy as jnp
import numpy as np
from jax import lax

C = 256
SIDE = 16
PER_PEER = 1
FR_DEV = 32
FRAMES = 4096
NCLIP = 512
MOST_LEN = 32
N_DP = 4
N_CHAN = 32


def draw_pack_dest(key, part):
    key = jax.random.fold_in(key, 7)
    block_total = N_DP * N_CHAN
    seed_keys = jax.random.split(key, block_total)

    def shuffle_one(single_key):
        return jax.random.permutation(single_key, FR_DEV).astype(jnp.int32)
    shuffled = jax.vmap(shuffle_one)(seed_keys)
    block_ids = jnp.arange(block_total, dtype=jnp.int32)[:, None]
    group_ids = block_ids // N_CHAN
    source_ids = block_ids % N_CHAN
    dest_blocks = group_ids * N_CHAN + shuffled // PER_PEER
    placed = dest_blocks * FR_DEV + source_ids * PER_PEER + shuffled % PER_PEER
    return placed.reshape(-1).astype(jnp.int32)


def raised(drawn, key, source, target, parts, factor):
    owner, partner = [(jnp.arange(drawn.shape[dim]) // (drawn.shape[dim] // parts)).reshape([-1 if axis == dim else 1 for axis in range(drawn.ndim)]) for dim in (source, target)]
    chosen = jax.random.permutation(key, parts)[partner]
    strong = (owner == chosen) | (owner == (partner + parts // 2) % parts)
    return jnp.where(strong, factor * drawn, drawn)


def levels(rng, extent, cuts, low, high):
    factor_of = 1.0
    for dim, blocks in cuts:
        heights = jax.random.uniform(jax.random.fold_in(jax.random.fold_in(rng, 6), dim), (blocks,), jnp.float32, low / len(cuts), high / len(cuts))
        factor_of = factor_of * jnp.repeat(jnp.exp(heights), extent[dim] // blocks).reshape((-1,) + (1,) * (len(extent) - 1 - dim))
    return factor_of


def split_up(count, total, bound, lean):
    portions = [(1 << 20) // math.isqrt(grade ** lean) + 1 for grade in range(2, count + 1)]
    spare, given = total - bound - (count - 1), [1] * (count - 1)
    while spare > 0:
        movable = [i for i in range(count - 1) if given[i] < bound]
        mass, budget = sum([portions[i] for i in movable]), spare
        for i in movable:
            more = min(bound - given[i], max(1, budget * portions[i] // mass), spare)
            given[i] = given[i] + more
            spare = spare - more
    return np.array([bound] + given)


def ragged_sizes(key, amount, total, bound, slope):
    if amount == 2:
        one = jax.random.randint(key, (), max(1, total - bound), min(bound, total - 1) + 1)
        return jnp.stack([one, total - one])
    sizes = jnp.asarray(split_up(amount, total, bound, slope), jnp.int32)
    pairs = (amount - 1) // 2
    source_of, taker = sizes[1:1 + 2 * pairs:2], sizes[2:2 + 2 * pairs:2]
    slack = jnp.minimum(source_of - 1, bound - taker)
    moved = jax.random.randint(jax.random.fold_in(key, 1), (pairs,), 0, 1 << 20) % (slack + 1)
    sizes = sizes.at[1:1 + 2 * pairs:2].set(source_of - moved).at[2:2 + 2 * pairs:2].set(taker + moved)
    return sizes[jax.random.permutation(jax.random.fold_in(key, 2), amount)]


def gaussian(own_key, shape, spread, most, cuts=(), kind=jnp.bfloat16):
    array = jax.random.normal(own_key, shape, jnp.float32) * spread
    if len(cuts) > 0:
        array = levels(own_key, shape, cuts, -0.22, 0.18) * array
    return jnp.clip(array, min=-most, max=most).astype(kind)


def bell_draw_with(rng, dims, deviation, bound, shards, heavy, kind=jnp.bfloat16):
    drawn = deviation * jax.random.normal(rng, dims, jnp.float32)
    if shards:
        drawn = drawn * levels(rng, dims, shards, -0.22, 0.18)
    return jnp.clip(raised(drawn, jax.random.fold_in(rng, 3), *heavy), -bound, bound).astype(kind)


def setup_inputs(seed: int = 0) -> dict:
    streams_of = jax.random.split(jax.random.key(seed), 9)
    loaded = gaussian(streams_of[0], (C, FRAMES, SIDE * SIDE), 1.0, 6.0, ((1, 128),))
    pack_dest = draw_pack_dest(jax.random.fold_in(streams_of[8], 71), 0)
    clip_lengths = ragged_sizes(streams_of[2], NCLIP, FRAMES, MOST_LEN, 2).astype(jnp.int32)
    weight_one = gaussian(streams_of[3], (12, C, C), (12 * C) ** -0.5, 0.109375, ((1, 32),))
    weight_two = gaussian(streams_of[4], (3, C, C), (3 * C) ** -0.5, 0.21875, ((1, 32),))
    weight_three = gaussian(streams_of[5], (3, C, C), (3 * C) ** -0.5, 0.21875, ((1, 32),))
    norm_gains = jnp.clip(jnp.exp(jax.random.uniform(streams_of[6], (3, C), jnp.float32, math.log(0.5), math.log(2.0))), 0.5, 2.0)
    latent_grad = bell_draw_with(streams_of[7], (C, FRAMES * SIDE * SIDE // 4), (1.0 / (FRAMES * SIDE * SIDE // 4) ** 0.5), 0.046875, ((1, 128),), (1, 0, 128, 5.5))
    return {"loaded": loaded, "pack_dest": pack_dest, "clip_lengths": clip_lengths, "weight_one": weight_one, "weight_two": weight_two, "weight_three": weight_three, "norm_gains": norm_gains, "latent_grad": latent_grad}


EPS = 1e-05

def clip_place(clip_lengths, total_frames):
    clip_ends = jnp.cumsum(clip_lengths).astype(jnp.int32)
    clip_starts = (clip_ends - clip_lengths).astype(jnp.int32)
    frame_ids = jnp.arange(total_frames, dtype=jnp.int32)
    inside = (frame_ids[:, None] >= clip_starts[None, :]) & (frame_ids[:, None] < clip_ends[None, :])
    return lax.optimization_barrier(jnp.sum(jnp.where(inside, frame_ids[:, None] - clip_starts[None, :], 0), axis=1)).astype(jnp.int32)

def earlier_frames(signal, lag_frames, clip_offset):
    if lag_frames > 0:
        padding = jnp.zeros((signal.shape[0], lag_frames, signal.shape[2]), signal.dtype)
        shifted = jnp.concatenate([padding, signal[:, :signal.shape[1] - lag_frames, :]], axis=1)
    else:
        shifted = signal
    return jnp.where((clip_offset >= lag_frames)[None, :, None], shifted, jnp.zeros_like(shifted))

def later_frames(signal, lag_frames, clip_offset):
    masked = jnp.where((clip_offset >= lag_frames)[None, :, None], signal, jnp.zeros_like(signal))
    if lag_frames == 0:
        return masked
    padding = jnp.zeros((signal.shape[0], lag_frames, signal.shape[2]), signal.dtype)
    return jnp.concatenate([masked[:, lag_frames:, :], padding], axis=1)

def patches(signal):
    chan_total, frame_total, _ = signal.shape
    half_side = SIDE // 2
    grouped = signal.reshape(chan_total, frame_total, half_side, 2, half_side, 2).transpose(3, 5, 0, 1, 2, 4)
    return grouped.reshape(4 * chan_total, frame_total, half_side * half_side)

def convolve(signal, weight, step_size, clip_offset):
    groups = weight.shape[0] // 3
    summed = jnp.zeros((C, signal.shape[1] * signal.shape[2]), jnp.float32)
    for tap_index in range(3):
        shifted = earlier_frames(signal, tap_index * step_size, clip_offset).reshape(groups, C, -1)
        for group_index in range(groups):
            summed = summed + jnp.dot(weight[tap_index * groups + group_index].T, shifted[group_index], preferred_element_type=jnp.float32)
    return summed

def kernel_grad(signal, grad_flat, groups, step_size, clip_offset):
    pieces = []
    for tap_index in range(3):
        shifted = earlier_frames(signal, tap_index * step_size, clip_offset).reshape(groups, C, -1)
        for group_index in range(groups):
            pieces.append(jnp.dot(shifted[group_index], grad_flat.T, preferred_element_type=jnp.float32))
    return jnp.stack(pieces)

def normalize(conv_out, total_frames):
    conv_frames = conv_out.reshape(C, total_frames, -1)
    frame_mean = lax.optimization_barrier(jnp.mean(conv_frames, axis=(0, 2)))
    frame_var = lax.optimization_barrier(jnp.mean(conv_frames * conv_frames, axis=(0, 2))) - frame_mean * frame_mean
    inv_scale = lax.rsqrt(frame_var + EPS)
    return ((conv_frames - frame_mean[None, :, None]) * inv_scale[None, :, None], inv_scale)

def reference(loaded, pack_dest, clip_lengths, weight_one, weight_two, weight_three, norm_gains, latent_grad):
    clip_offset = clip_place(clip_lengths, FRAMES)
    packed = jnp.zeros_like(loaded).at[:, pack_dest, :].set(loaded)
    weights = (weight_one, weight_two, weight_three)
    dilations = (1, 2, 4)
    current = packed
    saved = []
    for layer_index in range(3):
        signal = patches(current) if layer_index == 0 else current
        conv_out = convolve(signal, weights[layer_index], dilations[layer_index], clip_offset)
        normed, inv_scale = normalize(conv_out, FRAMES)
        scaled = norm_gains[layer_index][:, None, None] * normed
        current = jax.nn.silu(scaled).astype(jnp.bfloat16)
        saved.append((signal, conv_out))
    latent = current.reshape(C, -1)
    upstream = latent_grad.astype(jnp.float32).reshape(C, FRAMES, -1)
    weight_grads = [None, None, None]
    gain_grads = [None, None, None]
    for layer_index in (2, 1, 0):
        signal, conv_out = saved[layer_index]
        normed, inv_scale = normalize(conv_out, FRAMES)
        scaled = norm_gains[layer_index][:, None, None] * normed
        sigmoid_y = jax.nn.sigmoid(scaled)
        grad_scaled = upstream * sigmoid_y * (1.0 + scaled * (1.0 - sigmoid_y))
        gain_grads[layer_index] = lax.optimization_barrier(jnp.sum(grad_scaled * normed, axis=(1, 2)))
        grad_normed = grad_scaled * norm_gains[layer_index][:, None, None]
        mean_grad = lax.optimization_barrier(jnp.mean(grad_normed, axis=(0, 2)))
        mean_proj = lax.optimization_barrier(jnp.mean(grad_normed * normed, axis=(0, 2)))
        grad_conv = (inv_scale[None, :, None] * (grad_normed - mean_grad[None, :, None] - normed * mean_proj[None, :, None])).astype(jnp.bfloat16)
        grad_flat = grad_conv.reshape(C, -1)
        step_size = dilations[layer_index]
        weight = weights[layer_index]
        weight_grads[layer_index] = kernel_grad(signal, grad_flat, weight.shape[0] // 3, step_size, clip_offset)
        if layer_index > 0:
            summed = jnp.zeros((C, grad_flat.shape[1]), jnp.float32)
            for tap_index in range(3):
                moved = later_frames(grad_conv, tap_index * step_size, clip_offset).reshape(C, -1)
                summed = summed + jnp.dot(weight[tap_index], moved, preferred_element_type=jnp.float32)
            upstream = summed.reshape(C, FRAMES, -1)
    return (latent, weight_grads[0], weight_grads[1], weight_grads[2], jnp.stack(gain_grads))
```

```python
import functools
import jax
import jax.numpy as jnp
from jax import lax
from jax.experimental import pallas as pl
from jax.experimental.pallas import tpu as pltpu
from jax.sharding import PartitionSpec as P

SIDE = 16
CELLS = 64
C = 256
FR = 32
EPS = 1e-05
DILATIONS = (1, 2, 4)
CH = 8
F32 = jnp.float32
BF16 = jnp.bfloat16
MESH = pl.DeviceIdType.MESH
VMEM_SPEC = pl.BlockSpec(memory_space=pltpu.VMEM)
SMEM_SPEC = pl.BlockSpec(memory_space=pltpu.SMEM)
ANY_SPEC = pl.BlockSpec(memory_space=pl.ANY)
LIMIT = 60 << 20


def shifted(array, axis, by):
    peers = lax.axis_size(axis)
    pairs = [(i, i + by) for i in range(peers) if 0 <= i + by < peers]
    return lax.ppermute(array, axis, pairs)


def clip_place(clip_lengths, frame_ids):
    clip_ends = jnp.cumsum(clip_lengths)
    clip_starts = clip_ends - clip_lengths
    inside = (frame_ids[:, None] >= clip_starts[None, :]) & (
        frame_ids[:, None] < clip_ends[None, :]
    )
    return jnp.sum(jnp.where(inside, frame_ids[:, None] - clip_starts[None, :], 0), axis=1)


def sigmoid(value):
    return 0.5 * jnp.tanh(0.5 * value) + 0.5


def prep_kernel(order_ref, loaded_ref, pick_ref, out_ref, wide):
    for lane in range(2):
        for part in range(8):
            rows = pl.ds(part * 32, 32)
            block = loaded_ref[rows, :, lane * 128 : lane * 128 + 128]
            wide[lane, pl.ds(part * 1024, 1024), :] = block.astype(F32).reshape(1024, 128)

    @pl.loop(0, FR)
    def _(dest):
        frame = order_ref[dest]
        halves = [
            wide.at[lane][pl.ds(frame, C, stride=FR), :].astype(BF16) for lane in range(2)
        ]
        image = jnp.concatenate(halves, axis=1)
        cells = lax.dot_general(
            pick_ref[...], image, (((1,), (1,)), ((), ())), preferred_element_type=F32
        ).astype(BF16)
        for tap in range(4):
            out_ref[dest, :, tap * C : (tap + 1) * C] = cells[tap * CELLS : (tap + 1) * CELLS]


def prepare(order, loaded):
    cell = jnp.arange(SIDE * SIDE, dtype=jnp.int32)
    row, col = cell // SIDE, cell % SIDE
    place = (2 * (row % 2) + col % 2) * CELLS + (row // 2) * (SIDE // 2) + col // 2
    pick = (place[None, :] == cell[:, None]).astype(BF16)
    return pl.pallas_call(
        prep_kernel,
        out_shape=jax.ShapeDtypeStruct((FR, CELLS, 4 * C), BF16),
        in_specs=[SMEM_SPEC, VMEM_SPEC, VMEM_SPEC],
        out_specs=VMEM_SPEC,
        scratch_shapes=[pltpu.VMEM((2, C * FR, 128), F32)],
        compiler_params=pltpu.CompilerParams(vmem_limit_bytes=LIMIT),
    )(order, loaded, pick)


def place_of():
    x, chan = lax.axis_index("dp"), lax.axis_index("chan")
    return x, chan // 8, chan // 2 % 4, chan % 2


def chan_of(z, y, core):
    return z * 8 + y * 2 + core


def exchange_kernel(send, wblk, packed, full, send_sem, recv_sem, wsend, wrecv, hsem, lsem):
    x, z, y, core = place_of()
    chan = chan_of(z, y, core)
    chip = z * 4 + y
    offsets = [(dz, dy, dc) for dz in range(4) for dy in range(4) for dc in range(2)][1:]
    partner = [((z + dz) % 4, (y + dy) % 4, (core + dc) % 2) for dz, dy, dc in offsets]
    origin = [((z - dz) % 4, (y - dy) % 4, (core + dc) % 2) for dz, dy, dc in offsets]
    index = x * 32 + chan
    after, before = (index + 1) % 128, (index + 127) % 128
    after_id = (after // 32, after % 32)
    before_id = (before // 32, before % 32)

    barrier = pltpu.get_barrier_semaphore()
    for p in partner:
        pl.semaphore_signal(barrier, inc=1, device_id=(x, chan_of(*p)), device_id_type=MESH)
    for dx in (1, 2, 3):
        pl.semaphore_signal(barrier, inc=1, device_id=((x + dx) % 4, chan), device_id_type=MESH)
    pl.semaphore_signal(barrier, inc=1, device_id=after_id, device_id_type=MESH)
    pl.semaphore_signal(barrier, inc=1, device_id=before_id, device_id_type=MESH)
    pl.semaphore_wait(barrier, 31 + 3 + 2)

    def frame_copy(k):
        to = chan_of(*partner[k])
        return pltpu.make_async_remote_copy(
            src_ref=send.at[to], dst_ref=packed.at[chan + 2],
            send_sem=send_sem.at[k], recv_sem=recv_sem.at[k],
            device_id=(x, to), device_id_type=MESH,
        )

    def frame_wait(k):
        slot = packed.at[chan_of(*origin[k]) + 2]
        pltpu.make_async_remote_copy(
            src_ref=slot, dst_ref=slot, send_sem=send_sem.at[k], recv_sem=recv_sem.at[k],
            device_id=(x, chan), device_id_type=MESH,
        ).wait_recv()

    def part(taps, rows, lanes):
        return full.at[taps, rows, lanes]

    my_taps = pl.ds(5 * x, 5)
    my_lanes = pl.ds(pl.multiple_of(core * 128, 128), 128)
    my_rows = pl.ds(pl.multiple_of(chip * 16, 16), 16)
    my_plane = pl.ds(pl.multiple_of(z * 64, 64), 64)
    every = pl.ds(0, C)

    def remote(src, dst, n, device):
        return pltpu.make_async_remote_copy(
            src_ref=src, dst_ref=dst, send_sem=wsend.at[n], recv_sem=wrecv.at[n],
            device_id=device, device_id_type=MESH,
        )

    def wait_for(dst, n):
        remote(dst, dst, n, (x, chan)).wait_recv()

    mine = pltpu.make_async_copy(send.at[chan], packed.at[chan + 2], lsem.at[0])
    mine.start()
    local = pltpu.make_async_copy(
        wblk.at[my_taps, :, my_lanes], part(my_taps, my_rows, my_lanes), lsem.at[1]
    )
    local.start()
    copies = [frame_copy(k) for k in range(31)]
    stage_y = [
        remote(
            wblk.at[my_taps, :, my_lanes], part(my_taps, my_rows, my_lanes), d - 1,
            (x, chan_of(z, (y + d) % 4, core)),
        )
        for d in (1, 2, 3)
    ]
    for c in stage_y:
        c.start()
    for k in range(0, 8):
        copies[k].start()
    local.wait()
    for d in (1, 2, 3):
        rows = pl.ds(pl.multiple_of((z * 4 + (y - d) % 4) * 16, 16), 16)
        wait_for(part(my_taps, rows, my_lanes), d - 1)
    stage_z = [
        remote(
            part(my_taps, my_plane, my_lanes), part(my_taps, my_plane, my_lanes), 2 + d,
            (x, chan_of((z + d) % 4, y, core)),
        )
        for d in (1, 2, 3)
    ]
    for c in stage_z:
        c.start()
    for k in range(8, 16):
        copies[k].start()
    for d in (1, 2, 3):
        rows = pl.ds(pl.multiple_of((z - d) % 4 * 64, 64), 64)
        wait_for(part(my_taps, rows, my_lanes), 2 + d)
    stage_x = [
        remote(
            part(my_taps, every, my_lanes), part(my_taps, every, my_lanes), 5 + d,
            ((x + d) % 4, chan),
        )
        for d in (1, 2, 3)
    ]
    for c in stage_x:
        c.start()
    for k in range(16, 31):
        copies[k].start()
    for d in (1, 2, 3):
        wait_for(part(pl.ds(5 * ((x - d) % 4), 5), every, my_lanes), 5 + d)
    all_taps = pl.ds(0, 20)
    other = pl.ds(pl.multiple_of((1 - core) * 128, 128), 128)
    to_sister = remote(
        part(all_taps, every, my_lanes), part(all_taps, every, my_lanes), 9,
        (x, chan_of(z, y, 1 - core)),
    )
    to_sister.start()
    mine.wait()
    for k in range(31):
        frame_wait(k)
    tail = pltpu.make_async_remote_copy(
        src_ref=packed.at[pl.ds(FR, 2)], dst_ref=packed.at[pl.ds(0, 2)],
        send_sem=hsem.at[0], recv_sem=hsem.at[1], device_id=after_id, device_id_type=MESH,
    )
    tail.start()
    wait_for(part(all_taps, every, other), 9)
    for c in copies + stage_y + stage_z + stage_x + [to_sister]:
        c.wait_send()
    tail.wait()


def exchange(send, wblk):
    return pl.pallas_call(
        exchange_kernel,
        out_shape=(
            jax.ShapeDtypeStruct((FR + 2, CELLS, 4 * C), BF16),
            jax.ShapeDtypeStruct((20, C, C), BF16),
        ),
        in_specs=[ANY_SPEC, ANY_SPEC],
        out_specs=(ANY_SPEC, ANY_SPEC),
        scratch_shapes=[
            pltpu.SemaphoreType.DMA((31,)),
            pltpu.SemaphoreType.DMA((31,)),
            pltpu.SemaphoreType.DMA((10,)),
            pltpu.SemaphoreType.DMA((10,)),
            pltpu.SemaphoreType.DMA((2,)),
            pltpu.SemaphoreType.DMA((2,)),
        ],
        compiler_params=pltpu.CompilerParams(collective_id=0, has_side_effects=True),
    )(send, wblk)


def conv_norm(layer, src, weights, mask, gains, norm, inv, emit):
    step = DILATIONS[layer]
    gain = gains[layer : layer + 1, :].reshape(1, 1, C)

    @pl.loop(0, FR // CH)
    def _(chunk):
        start = chunk * CH
        conv = None
        for tap in range(3):
            rows = src[pl.ds(start + (2 - tap) * step, CH)].reshape(CH * CELLS, -1)
            term = jnp.dot(rows, weights(tap), preferred_element_type=F32)
            term = term.reshape(CH, CELLS, C)
            if tap == 0:
                conv = term
            else:
                conv = conv + term * mask[2 * layer + tap - 1, pl.ds(start, CH)]
        mean = jnp.sum(conv, axis=(1, 2), keepdims=True) * (1.0 / (CELLS * C))
        square = jnp.sum(conv * conv, axis=(1, 2), keepdims=True) * (1.0 / (CELLS * C))
        scale = lax.rsqrt(square - mean * mean + EPS)
        normed = (conv - mean) * scale
        norm[pl.ds(start, CH)] = normed
        inv[pl.ds(start, CH)] = jnp.broadcast_to(scale, (CH, 1, C))
        scaled = gain * normed
        emit(chunk, (scaled * sigmoid(scaled)).astype(BF16))


def norm_back(layer, upstream, mask, gains, norm, inv, gain_grad, grad, masked):
    gain = gains[layer : layer + 1, :].reshape(1, 1, C)
    gain_grad[...] = jnp.zeros_like(gain_grad)

    @pl.loop(0, FR // CH)
    def _(chunk):
        start = chunk * CH
        normed = norm[pl.ds(start, CH)]
        scaled = gain * normed
        sig = sigmoid(scaled)
        scaled_grad = upstream(chunk) * sig * (1.0 + scaled * (1.0 - sig))
        gain_grad[0:1, :] += jnp.sum(scaled_grad * normed, axis=(0, 1), keepdims=True)[0]
        normed_grad = scaled_grad * gain
        m1 = jnp.sum(normed_grad, axis=(1, 2), keepdims=True) * (1.0 / (CELLS * C))
        m2 = jnp.sum(normed_grad * normed, axis=(1, 2), keepdims=True) * (1.0 / (CELLS * C))
        result = inv[pl.ds(start, CH)] * (normed_grad - m1 - normed * m2)
        rounded = result.astype(BF16)
        grad[pl.ds(start, CH)] = rounded
        for tap in (1, 2):
            keep = mask[2 * layer + tap - 1, pl.ds(start, CH)]
            masked[tap - 1, pl.ds(start, CH)] = (rounded.astype(F32) * keep).astype(BF16)


def weight_grad(layer, src, grad, masked, out, groups):
    step = DILATIONS[layer]
    for tap in range(3):
        if tap == 0:
            right = grad[...].reshape(FR * CELLS, C)
        else:
            right = masked[tap - 1].reshape(FR * CELLS, C)
        for group in range(groups):
            left = src[pl.ds((2 - tap) * step, FR), :, group * C : (group + 1) * C]
            out[tap * groups + group] = lax.dot_general(
                left.reshape(FR * CELLS, C), right, (((0,), (0,)), ((), ())),
                preferred_element_type=F32,
            )


def input_grad(layer, extended, weights, mask):
    step = DILATIONS[layer]

    def chunk_grad(chunk):
        start = chunk * CH
        total = None
        for tap in range(3):
            rows = extended[pl.ds(start + tap * step, CH)].reshape(CH * CELLS, C)
            term = lax.dot_general(
                rows, weights[tap], (((1,), (1,)), ((), ())), preferred_element_type=F32
            ).reshape(CH, CELLS, C)
            if tap == 0:
                total = term
            else:
                total = total + term * mask[2 * layer + tap - 1, pl.ds(start + tap * step, CH)]
        return total

    return chunk_grad


def first_kernel(src, weights, mask, gains, norm, inv, act):
    def emit(chunk, value):
        act[pl.ds(chunk * CH, CH)] = value

    conv_norm(
        0, src, lambda tap: weights[4 * tap : 4 * tap + 4].reshape(4 * C, C), mask, gains,
        norm, inv, emit,
    )


def second_kernel(early, src, weights, mask, gains, norm, inv, act, extended):
    extended[0:4] = early[...]
    extended[4:] = src[...]

    def emit(chunk, value):
        act[pl.ds(chunk * CH, CH)] = value

    conv_norm(1, extended, lambda tap: weights[12 + tap], mask, gains, norm, inv, emit)


def third_kernel(
    early, src, weights, mask, gains, cotangent, latent, grad, wgrad, gain_grad,
    extended, norm, inv, masked,
):
    extended[0:8] = early[...]
    extended[8:] = src[...]

    def emit(chunk, value):
        lanes = pl.ds(pl.multiple_of(chunk * CH * CELLS, CH * CELLS), CH * CELLS)
        latent[:, lanes] = value.reshape(CH * CELLS, C).T

    conv_norm(2, extended, lambda tap: weights[15 + tap], mask, gains, norm, inv, emit)

    def upstream(chunk):
        lanes = pl.ds(pl.multiple_of(chunk * CH * CELLS, CH * CELLS), CH * CELLS)
        return cotangent[:, lanes].T.astype(F32).reshape(CH, CELLS, C)

    norm_back(2, upstream, mask, gains, norm, inv, gain_grad, grad, masked)
    weight_grad(2, extended, grad, masked, wgrad, 1)


def back_second_kernel(
    late, later_grad, early, src, weights, mask, gains, norm, inv, grad, wgrad, gain_grad,
    extended, joined, masked,
):
    extended[0:4] = early[...]
    extended[4:] = src[...]
    joined[0:FR] = later_grad[...]
    joined[FR:] = late[...]
    upstream = input_grad(2, joined, weights.at[15:18], mask)
    norm_back(1, upstream, mask, gains, norm, inv, gain_grad, grad, masked)
    weight_grad(1, extended, grad, masked, wgrad, 1)


def back_first_kernel(
    late, later_grad, src, weights, mask, gains, norm, inv, wgrad, gain_grad,
    joined, grad, masked,
):
    joined[0:FR] = later_grad[...]
    joined[FR:] = late[...]
    upstream = input_grad(1, joined, weights.at[12:15], mask)
    norm_back(0, upstream, mask, gains, norm, inv, gain_grad, grad, masked)
    weight_grad(0, src, grad, masked, wgrad, 4)


def on_device(kernel, outs, scratch, args):
    return pl.pallas_call(
        kernel,
        out_shape=tuple(jax.ShapeDtypeStruct(shape, kind) for shape, kind in outs),
        in_specs=[VMEM_SPEC] * len(args),
        out_specs=(VMEM_SPEC,) * len(outs),
        scratch_shapes=[pltpu.VMEM(shape, kind) for shape, kind in scratch],
        compiler_params=pltpu.CompilerParams(vmem_limit_bytes=LIMIT),
    )(*args)


def reduce_kernel(
    one, two, three, gain_one, gain_two, gain_three, out_one, out_two, out_three, gains,
    sister_out, sister_in, chip_sum, plane_in, row_out, row_in, total, last_in,
    gain_sister, gain_chip, gain_plane, gain_row, send_sem, recv_sem,
):
    x, z, y, core = place_of()
    chan = chan_of(z, y, core)
    chip = z * 4 + y
    sister = (x, chan_of(z, y, 1 - core))
    offsets = [(dz, dy) for dz in range(4) for dy in range(4)][1:]
    partner = [(x, chan_of((z + dz) % 4, (y + dy) % 4, core)) for dz, dy in offsets]
    row = [((x + d) % 4, chan) for d in (1, 2, 3)]

    barrier = pltpu.get_barrier_semaphore()
    for device in [sister] + partner + row:
        pl.semaphore_signal(barrier, inc=1, device_id=device, device_id_type=MESH)
    pl.semaphore_wait(barrier, 19)

    def remote(src, dst, n, device):
        return pltpu.make_async_remote_copy(
            src_ref=src, dst_ref=dst, send_sem=send_sem.at[n], recv_sem=recv_sem.at[n],
            device_id=device, device_id_type=MESH,
        )

    def wait_for(dst, n):
        remote(dst, dst, n, (x, chan)).wait_recv()

    started = []

    def go(copy):
        copy.start()
        started.append(copy)

    low = core == 0
    gain_chip[...] = jnp.zeros_like(gain_chip)
    for n, part in enumerate((gain_one, gain_two, gain_three)):
        gain_chip[n : n + 1, :] = part[0:1, :]
    go(remote(gain_chip, gain_sister, 0, sister))

    pieces = [(two, 0, 3, 12), (three, 0, 3, 15), (one, 0, 6, 0), (one, 6, 6, 6)]
    for n, (ref, first, count, at) in enumerate(pieces):
        @pl.loop(0, count)
        def _(k, ref=ref, first=first, at=at):
            sister_out[at + k] = jnp.where(
                low, ref[first + k, :, 128:], ref[first + k, :, :128]
            ).astype(BF16)

        taps = pl.ds(at, count)
        go(remote(sister_out.at[taps], sister_in.at[taps], 1 + n, sister))
    wait_for(gain_sister, 0)
    for n, (ref, first, count, at) in enumerate(pieces):
        wait_for(sister_in.at[pl.ds(at, count)], 1 + n)

        @pl.loop(0, count)
        def _(k, ref=ref, first=first, at=at):
            own = jnp.where(low, ref[first + k, :, :128], ref[first + k, :, 128:])
            chip_sum[at + k] = (own + sister_in[at + k].astype(F32)).astype(BF16)

    my_rows = pl.ds(pl.multiple_of(chip * 16, 16), 16)
    for k, (dz, dy) in enumerate(offsets):
        to = (z + dz) % 4 * 4 + (y + dy) % 4
        rows = pl.ds(pl.multiple_of(to * 16, 16), 16)
        go(remote(chip_sum.at[:, rows, :], plane_in.at[k], 5 + k, partner[k]))
    started[0].wait_send()
    gain_plane[chip] = gain_chip[...] + gain_sister[...]
    for k in range(15):
        go(remote(gain_plane.at[chip], gain_plane.at[chip], 20 + k, partner[k]))

    for k in range(15):
        wait_for(plane_in.at[k], 5 + k)

    @pl.loop(0, 18)
    def _(tap):
        value = chip_sum[tap, my_rows, :].astype(F32)
        for k in range(15):
            value = value + plane_in[k, tap].astype(F32)
        total[tap] = value
        row_out[tap] = value.astype(BF16)

    for k in range(3):
        go(remote(row_out, row_in.at[k], 35 + k, row[k]))
    for k, (dz, dy) in enumerate(offsets):
        wait_for(gain_plane.at[(z - dz) % 4 * 4 + (y - dy) % 4], 20 + k)
    gain_total = gain_plane[0]
    for k in range(1, 16):
        gain_total = gain_total + gain_plane[k]
    gain_row[x] = gain_total
    for k in range(3):
        go(remote(gain_row.at[x], gain_row.at[x], 38 + k, row[k]))
    for k in range(3):
        wait_for(row_in.at[k], 35 + k)

    @pl.loop(0, 18)
    def _(tap):
        value = total[tap]
        for k in range(3):
            value = value + row_in[k, tap].astype(F32)
        total[tap] = value

    theirs = pl.ds(pl.multiple_of((1 - core) * 8, 8), 8)
    ours = pl.ds(pl.multiple_of(core * 8, 8), 8)
    go(remote(total.at[:, theirs, :], last_in, 41, sister))
    for k, d in enumerate((1, 2, 3)):
        wait_for(gain_row.at[(x - d) % 4], 38 + k)
    gains[...] = ((gain_row[0] + gain_row[1]) + gain_row[2]) + gain_row[3]
    wait_for(last_in, 41)
    for ref, at, count in ((out_one, 0, 12), (out_two, 12, 3), (out_three, 15, 3)):
        mine = total[at : at + count, ours, :]
        other = last_in[at : at + count]
        ref[:, :, :128] = jnp.where(low, mine, other)
        ref[:, :, 128:] = jnp.where(low, other, mine)
    for copy in started[1:]:
        copy.wait_send()


def reduce_all(*parts):
    return pl.pallas_call(
        reduce_kernel,
        out_shape=(
            jax.ShapeDtypeStruct((12, 8, C), F32),
            jax.ShapeDtypeStruct((3, 8, C), F32),
            jax.ShapeDtypeStruct((3, 8, C), F32),
            jax.ShapeDtypeStruct((8, C), F32),
        ),
        in_specs=[VMEM_SPEC] * 6,
        out_specs=(VMEM_SPEC,) * 4,
        scratch_shapes=[
            pltpu.VMEM((18, C, 128), BF16),
            pltpu.VMEM((18, C, 128), BF16),
            pltpu.VMEM((18, C, 128), BF16),
            pltpu.VMEM((15, 18, 16, 128), BF16),
            pltpu.VMEM((18, 16, 128), BF16),
            pltpu.VMEM((3, 18, 16, 128), BF16),
            pltpu.VMEM((18, 16, 128), F32),
            pltpu.VMEM((18, 8, 128), F32),
            pltpu.VMEM((8, C), F32),
            pltpu.VMEM((8, C), F32),
            pltpu.VMEM((16, 8, C), F32),
            pltpu.VMEM((4, 8, C), F32),
            pltpu.SemaphoreType.DMA((42,)),
            pltpu.SemaphoreType.DMA((42,)),
        ],
        compiler_params=pltpu.CompilerParams(
            collective_id=1, has_side_effects=True, vmem_limit_bytes=LIMIT
        ),
    )(*parts)


def shards(
    loaded, pack_dest, clip_lengths, weight_one, weight_two, weight_three, norm_gains, latent_grad
):
    block_index = lax.axis_index("dp") * 32 + lax.axis_index("chan")
    core = lax.axis_index("chan") % 2
    slots = jnp.arange(FR, dtype=jnp.int32)
    send_slot = pack_dest // FR % 32
    order = jnp.sum(jnp.where(send_slot[None, :] == slots[:, None], slots[None, :], 0), axis=1)
    own = jnp.concatenate(
        [weight_one, weight_two, weight_three, jnp.zeros((2, 8, C), BF16)], axis=0
    )
    pairs = [(i, i ^ 1) for i in range(32)]
    theirs = lax.ppermute(own, "chan", pairs)
    wblk = jnp.where(
        core == 0,
        jnp.concatenate([own, theirs], axis=1),
        jnp.concatenate([theirs, own], axis=1),
    )
    frame_ids = block_index * FR + jnp.arange(FR + 8, dtype=jnp.int32)
    offset = clip_place(clip_lengths, frame_ids)
    lags = jnp.array([1, 2, 2, 4, 4, 8], jnp.int32)
    mask = jnp.broadcast_to(
        (offset[None, :] >= lags[:, None]).astype(F32)[:, :, None, None], (6, FR + 8, 1, C)
    )
    send = prepare(order, loaded)
    packed, weights = exchange(send, wblk)

    image = (FR, CELLS, C)
    stat = (FR, 1, C)
    gain_row = ((8, C), F32)
    ring = ("dp", "chan")
    norm_one, inv_one, act_one = on_device(
        first_kernel, [(image, F32), (stat, F32), (image, BF16)], [],
        (packed, weights, mask, norm_gains),
    )
    early_one = shifted(act_one[FR - 4 :], ring, 1)
    norm_two, inv_two, act_two = on_device(
        second_kernel, [(image, F32), (stat, F32), (image, BF16)],
        [((FR + 4, CELLS, C), BF16)],
        (early_one, act_one, weights, mask, norm_gains),
    )
    early_two = shifted(act_two[FR - 8 :], ring, 1)
    masked = ((2,) + image, BF16)
    latent, grad_three, wgrad_three, gain_three = on_device(
        third_kernel,
        [((C, FR * CELLS), BF16), (image, BF16), ((3, C, C), F32), gain_row],
        [((FR + 8, CELLS, C), BF16), (image, F32), (stat, F32), masked],
        (early_two, act_two, weights, mask, norm_gains, latent_grad),
    )
    late_three = shifted(grad_three[:8], ring, -1)
    grad_two, wgrad_two, gain_two = on_device(
        back_second_kernel,
        [(image, BF16), ((3, C, C), F32), gain_row],
        [((FR + 4, CELLS, C), BF16), ((FR + 8, CELLS, C), BF16), masked],
        (late_three, grad_three, early_one, act_one, weights, mask, norm_gains, norm_two, inv_two),
    )
    late_two = shifted(grad_two[:4], ring, -1)
    wgrad_one, gain_one = on_device(
        back_first_kernel,
        [((12, C, C), F32), gain_row],
        [((FR + 4, CELLS, C), BF16), (image, BF16), masked],
        (late_two, grad_two, packed, weights, mask, norm_gains, norm_one, inv_one),
    )
    out_one, out_two, out_three, gains = reduce_all(
        wgrad_one, wgrad_two, wgrad_three, gain_one, gain_two, gain_three
    )
    return (latent, out_one, out_two, out_three, gains[:3])


def solution(mesh):
    placed = (
        P(None, ("dp", "chan"), None),
        P(("dp", "chan")),
        P(),
        P(None, "chan", None),
        P(None, "chan", None),
        P(None, "chan", None),
        P(),
        P(None, ("dp", "chan")),
    )
    return jax.shard_map(
        shards,
        mesh=mesh,
        in_specs=placed,
        out_specs=(
            P(None, ("dp", "chan")),
            P(None, "chan", None),
            P(None, "chan", None),
            P(None, "chan", None),
            P(),
        ),
        check_vma=False,
    )
```

```python
import functools
import jax
import jax.numpy as jnp
from jax import lax
from jax.experimental import pallas as pl
from jax.experimental.pallas import tpu as pltpu
from jax.sharding import PartitionSpec as P

SIDE = 16
CELLS = 64
C = 256
FR = 32
EPS = 1e-05
DILATIONS = (1, 2, 4)
CH = 8
F32 = jnp.float32
BF16 = jnp.bfloat16
MESH = pl.DeviceIdType.MESH
VMEM_SPEC = pl.BlockSpec(memory_space=pltpu.VMEM)
SMEM_SPEC = pl.BlockSpec(memory_space=pltpu.SMEM)
LIMIT = 60 << 20


def clip_place(clip_lengths, frame_ids):
    clip_ends = jnp.cumsum(clip_lengths)
    clip_starts = clip_ends - clip_lengths
    inside = (frame_ids[:, None] >= clip_starts[None, :]) & (
        frame_ids[:, None] < clip_ends[None, :]
    )
    return jnp.sum(jnp.where(inside, frame_ids[:, None] - clip_starts[None, :], 0), axis=1)


def sigmoid(value):
    return 0.5 * jnp.tanh(0.5 * value) + 0.5


ORDER = (
    (0, 1), (3, 0), (0, 3), (1, 0), (1, 1), (3, 3), (1, 3), (3, 1),
    (0, 2), (2, 0), (2, 2), (1, 2), (2, 3), (3, 2), (2, 1),
)
FRAME_OFFSETS = (
    tuple((dz, dy, 0) for dz, dy in ORDER)
    + ((0, 0, 1),)
    + tuple((dz, dy, 1) for dz, dy in ORDER)
    + ((0, 0, 0),)
)
GROUPS = ((15, 3), (12, 3), (0, 4), (4, 4), (8, 4))
NG = len(GROUPS)
PER_GROUP = 20
GAIN_AT = NG * PER_GROUP
HALO_AT = GAIN_AT + 19
WEIGHT_AT = HALO_AT + 6
FRAME_AT = WEIGHT_AT + 11
N_SEM = FRAME_AT + 31


def mean_of(value):
    return jnp.sum(value, axis=(1, 2), keepdims=True) * (1.0 / (CELLS * C))


def kernel(
    order, loaded, own, mask, gains, cotangent,
    latent, out_one, out_two, out_three, gain_out,
    wide, send, packed, full, own_f32, theirs_f32, wblk,
    conv_one, early_conv, late_conv, ext_two, ext_three, norm_two,
    inv_one, inv_two, g_one, g_two, g_three, masked, gain_sum,
    wacc, sister_out, sister_in, chip_sum, plane_in, row_out, row_in, total, last_in,
    gain_sister, gain_plane, gain_row, send_sem, recv_sem, local_sem,
):
    x, chan = lax.axis_index("dp"), lax.axis_index("chan")
    z, y, core = chan // 8, chan // 2 % 4, chan % 2
    chip = z * 4 + y
    low = core == 0

    def at_chan(zz, yy, cc):
        return zz * 8 + yy * 2 + cc

    index = x * 32 + chan
    after, before = (index + 1) % 128, (index + 127) % 128
    after_id = (after // 32, after % 32)
    before_id = (before // 32, before % 32)
    sister = (x, at_chan(z, y, 1 - core))
    plane = [(x, at_chan((z + dz) % 4, (y + dy) % 4, core)) for dz, dy in ORDER]
    row = [((x + d) % 4, chan) for d in (1, 2, 3)]
    partner = [
        at_chan((z + dz) % 4, (y + dy) % 4, (core + dc) % 2) for dz, dy, dc in FRAME_OFFSETS
    ]
    origin = [
        at_chan((z - dz) % 4, (y - dy) % 4, (core + dc) % 2) for dz, dy, dc in FRAME_OFFSETS
    ]

    barrier = pltpu.get_barrier_semaphore()
    for device in [(x, p) for p in partner[:31]] + row + [after_id, before_id]:
        pl.semaphore_signal(barrier, inc=1, device_id=device, device_id_type=MESH)

    started = []

    def remote(src, dst, n, device):
        return pltpu.make_async_remote_copy(
            src_ref=src, dst_ref=dst, send_sem=send_sem.at[n], recv_sem=recv_sem.at[n],
            device_id=device, device_id_type=MESH,
        )

    def go(src, dst, n, device):
        copy = remote(src, dst, n, device)
        copy.start()
        started.append(copy)

    def wait_for(dst, n):
        remote(dst, dst, n, (x, chan)).wait_recv()

    own_f32[...] = own[...].astype(F32)
    cells_in = lax.broadcasted_iota(jnp.int32, (SIDE * SIDE, SIDE * SIDE), 1)
    cells_out = lax.broadcasted_iota(jnp.int32, (SIDE * SIDE, SIDE * SIDE), 0)
    in_row, in_col = cells_in // SIDE, cells_in % SIDE
    place = (2 * (in_row % 2) + in_col % 2) * CELLS + (in_row // 2) * (SIDE // 2) + in_col // 2
    pick = jnp.where(place == cells_out, 1.0, 0.0).astype(BF16)
    pl.semaphore_wait(barrier, 36)
    go(own_f32, theirs_f32, WEIGHT_AT, sister)

    @pl.loop(0, 8)
    def _(part):
        rows = pl.ds(part * 32, 32)
        out_rows = pl.ds(pl.multiple_of(part * 1024, 1024), 1024)
        for lane in range(2):
            block = loaded[rows, :, lane * 128 : lane * 128 + 128]
            wide[lane, out_rows, :] = block.astype(F32).reshape(1024, 128)

    def image_of(dest):
        frame = order[dest]
        halves = [
            wide.at[lane][pl.ds(frame, C, stride=FR), :].astype(BF16) for lane in range(2)
        ]
        cells = lax.dot_general(
            pick, jnp.concatenate(halves, axis=1), (((1,), (1,)), ((), ())),
            preferred_element_type=F32,
        ).astype(BF16)
        return jnp.concatenate(
            [cells[tap * CELLS : (tap + 1) * CELLS] for tap in range(4)], axis=1
        )

    def send_frames(first, last):
        for k in range(first, last):
            send[k] = image_of(partner[k])
            go(send.at[k], packed.at[chan], FRAME_AT + k, (x, partner[k]))

    my_taps = pl.ds(5 * x, 5)
    my_lanes = pl.ds(pl.multiple_of(core * 128, 128), 128)
    other_lanes = pl.ds(pl.multiple_of((1 - core) * 128, 128), 128)
    my_rows = pl.ds(pl.multiple_of(chip * 16, 16), 16)
    my_plane = pl.ds(pl.multiple_of(z * 64, 64), 64)

    send_frames(0, 4)
    wait_for(theirs_f32, WEIGHT_AT)
    mine_w, their_w = own_f32[...], theirs_f32[...]
    wblk[...] = jnp.concatenate(
        [jnp.where(low, mine_w, their_w), jnp.where(low, their_w, mine_w)], axis=1
    ).astype(BF16)
    local = pltpu.make_async_copy(
        wblk.at[my_taps, :, my_lanes], full.at[my_taps, my_rows, my_lanes], local_sem
    )
    local.start()
    for d in (1, 2, 3):
        go(
            wblk.at[my_taps, :, my_lanes], full.at[my_taps, my_rows, my_lanes],
            WEIGHT_AT + d, (x, at_chan(z, (y + d) % 4, core)),
        )
    send_frames(4, 8)
    local.wait()
    for d in (1, 2, 3):
        rows = pl.ds(pl.multiple_of((z * 4 + (y - d) % 4) * 16, 16), 16)
        wait_for(full.at[my_taps, rows, my_lanes], WEIGHT_AT + d)
    block = full.at[my_taps, my_plane, my_lanes]
    for d in (1, 2, 3):
        go(block, block, WEIGHT_AT + 3 + d, (x, at_chan((z + d) % 4, y, core)))
    send_frames(8, 14)
    for d in (1, 2, 3):
        rows = pl.ds(pl.multiple_of((z - d) % 4 * 64, 64), 64)
        wait_for(full.at[my_taps, rows, my_lanes], WEIGHT_AT + 3 + d)
    block = full.at[my_taps, :, my_lanes]
    for d in (1, 2, 3):
        go(block, block, WEIGHT_AT + 6 + d, row[d - 1])
    send_frames(14, 31)
    packed[chan] = image_of(chan)
    for d in (1, 2, 3):
        wait_for(full.at[pl.ds(5 * ((x - d) % 4), 5), :, my_lanes], WEIGHT_AT + 6 + d)
    block = full.at[:, :, my_lanes]
    go(block, block, WEIGHT_AT + 10, sister)
    wait_for(full.at[:, :, other_lanes], WEIGHT_AT + 10)

    conv_one[...] = jnp.zeros_like(conv_one)

    def add_products(batch):
        slots = []
        for k in batch:
            if k < 31:
                wait_for(packed.at[origin[k]], FRAME_AT + k)
            slots.append(origin[k])
        rows = jnp.concatenate([packed[s] for s in slots], axis=0)
        for tap in range(3):
            term = jnp.dot(
                rows, full[4 * tap : 4 * tap + 4].reshape(4 * C, C), preferred_element_type=F32
            )
            for n, s in enumerate(slots):
                piece = term[n * CELLS : (n + 1) * CELLS]
                if tap > 0:
                    piece = piece * mask[tap - 1, s + tap]
                conv_one[s + tap] += piece

    for first in range(0, 32, 8):
        add_products(range(first, first + 8))
    late_conv[...] = conv_one[FR:]
    go(late_conv, early_conv, HALO_AT, after_id)

    def gain_of(layer):
        return gains[layer : layer + 1, :].reshape(1, 1, C)

    def normalize(conv):
        mean = mean_of(conv)
        scale = lax.rsqrt(mean_of(conv * conv) - mean * mean + EPS)
        return (conv - mean) * scale, jnp.broadcast_to(scale, (conv.shape[0], 1, C))

    def conv_of(layer, src, first, start):
        step = DILATIONS[layer]
        conv = None
        for tap in range(3):
            rows = src[pl.ds(start + (2 - tap) * step, CH)].reshape(CH * CELLS, C)
            term = jnp.dot(rows, full[first + tap], preferred_element_type=F32)
            term = term.reshape(CH, CELLS, C)
            if tap == 0:
                conv = term
            else:
                conv = conv + term * mask[2 * layer + tap - 1, pl.ds(start, CH)]
        return conv

    @pl.loop(0, FR // CH)
    def _(i):
        start = (FR // CH - 1 - i) * CH

        @pl.when(i == FR // CH - 1)
        def _():
            wait_for(early_conv, HALO_AT)
            conv_one[0:2] += early_conv[...]

        normed, scale = normalize(conv_one[pl.ds(start, CH)])
        conv_one[pl.ds(start, CH)] = normed
        inv_one[pl.ds(start, CH)] = scale
        scaled = gain_of(0) * normed
        ext_two[pl.ds(start + 4, CH)] = (scaled * sigmoid(scaled)).astype(BF16)

        @pl.when(i == 0)
        def _():
            remote(ext_two.at[FR :], ext_two.at[0:4], HALO_AT + 1, after_id).start()

    @pl.loop(0, FR // CH)
    def _(i):
        start = (FR // CH - 1 - i) * CH

        @pl.when(i == FR // CH - 1)
        def _():
            wait_for(ext_two.at[0:4], HALO_AT + 1)

        normed, scale = normalize(conv_of(1, ext_two, 12, start))
        norm_two[pl.ds(start, CH)] = normed
        inv_two[pl.ds(start, CH)] = scale
        scaled = gain_of(1) * normed
        ext_three[pl.ds(start + 8, CH)] = (scaled * sigmoid(scaled)).astype(BF16)

        @pl.when(i == 0)
        def _():
            remote(ext_three.at[FR :], ext_three.at[0:8], HALO_AT + 2, after_id).start()

    def norm_back(layer, upstream, normed, scale):
        gain = gain_of(layer)
        scaled = gain * normed
        sig = sigmoid(scaled)
        scaled_grad = upstream * sig * (1.0 + scaled * (1.0 - sig))
        gain_sum[layer : layer + 1, :] += jnp.sum(
            scaled_grad * normed, axis=(0, 1), keepdims=True
        )[0]
        normed_grad = scaled_grad * gain
        m1 = mean_of(normed_grad)
        m2 = mean_of(normed_grad * normed)
        return (scale * (normed_grad - m1 - normed * m2)).astype(BF16)

    def keep_masked(layer, start, value):
        for tap in (1, 2):
            kept = value.astype(F32) * mask[2 * layer + tap - 1, pl.ds(start, CH)]
            masked[tap - 1, pl.ds(start, CH)] = kept.astype(BF16)

    gain_sum[...] = jnp.zeros_like(gain_sum)

    @pl.loop(0, FR // CH)
    def _(i):
        start = (FR // CH - 1 - i) * CH

        @pl.when(i == FR // CH - 1)
        def _():
            wait_for(ext_three.at[0:8], HALO_AT + 2)

        normed, scale = normalize(conv_of(2, ext_three, 15, start))
        scaled = gain_of(2) * normed
        act = scaled * sigmoid(scaled)
        lanes = pl.ds(pl.multiple_of(start * CELLS, CH * CELLS), CH * CELLS)
        latent[:, lanes] = act.reshape(CH * CELLS, C).T.astype(BF16)
        upstream = cotangent[:, lanes].astype(F32).T.reshape(CH, CELLS, C)
        value = norm_back(2, upstream, normed, scale)
        g_three[pl.ds(start, CH)] = value
        keep_masked(2, start, value)

    go(g_three.at[0:8], g_three.at[FR :], HALO_AT + 3, before_id)

    def weight_grad(layer, src, at, grad):
        step = DILATIONS[layer]
        for tap in range(3):
            right = grad[0:FR] if tap == 0 else masked[tap - 1, 0:FR]
            left = src[pl.ds((2 - tap) * step, FR)].reshape(FR * CELLS, C)
            wacc[at + tap] = lax.dot_general(
                left, right.reshape(FR * CELLS, C), (((0,), (0,)), ((), ())),
                preferred_element_type=F32,
            )

    def to_sister(g):
        at, count = GROUPS[g]
        for k in range(at, at + count):
            sister_out[k] = jnp.where(low, wacc[k, :, 128:], wacc[k, :, :128]).astype(BF16)
        taps = pl.ds(at, count)
        go(sister_out.at[taps], sister_in.at[taps], g * PER_GROUP, sister)

    def to_plane(g):
        at, count = GROUPS[g]
        taps = pl.ds(at, count)
        wait_for(sister_in.at[taps], g * PER_GROUP)
        for k in range(at, at + count):
            mine = jnp.where(low, wacc[k, :, :128], wacc[k, :, 128:])
            chip_sum[k] = (mine + sister_in[k].astype(F32)).astype(BF16)
        for k, (dz, dy) in enumerate(ORDER):
            to = (z + dz) % 4 * 4 + (y + dy) % 4
            rows = pl.ds(pl.multiple_of(to * 16, 16), 16)
            go(
                chip_sum.at[taps, rows, :], plane_in.at[k, taps], g * PER_GROUP + 1 + k, plane[k]
            )

    def to_row(g):
        at, count = GROUPS[g]
        taps = pl.ds(at, count)
        value = chip_sum[taps, my_rows, :].astype(F32)
        for k in range(15):
            wait_for(plane_in.at[k, taps], g * PER_GROUP + 1 + k)
            value = value + plane_in[k, taps].astype(F32)
        total[taps] = value
        row_out[taps] = value.astype(BF16)
        for k in range(3):
            go(row_out.at[taps], row_in.at[k, taps], g * PER_GROUP + 16 + k, row[k])

    their_rows = pl.ds(pl.multiple_of((1 - core) * 8, 8), 8)
    our_rows = pl.ds(pl.multiple_of(core * 8, 8), 8)

    def to_owner(g):
        at, count = GROUPS[g]
        taps = pl.ds(at, count)
        value = total[taps]
        for k in range(3):
            wait_for(row_in.at[k, taps], g * PER_GROUP + 16 + k)
            value = value + row_in[k, taps].astype(F32)
        total[taps] = value
        go(total.at[taps, their_rows, :], last_in.at[taps], g * PER_GROUP + 19, sister)

    weight_grad(2, ext_three, 15, g_three)
    to_sister(0)

    def input_grad(layer, src, first, start):
        step = DILATIONS[layer]
        grad = None
        for tap in range(3):
            rows = src[pl.ds(start + tap * step, CH)].reshape(CH * CELLS, C)
            term = lax.dot_general(
                rows, full[first + tap], (((1,), (1,)), ((), ())), preferred_element_type=F32
            ).reshape(CH, CELLS, C)
            if tap == 0:
                grad = term
            else:
                grad = grad + term * mask[2 * layer + tap - 1, pl.ds(start + tap * step, CH)]
        return grad

    @pl.loop(0, FR // CH)
    def _(i):
        start = i * CH

        @pl.when(i == FR // CH - 1)
        def _():
            wait_for(g_three.at[FR :], HALO_AT + 3)

        value = norm_back(
            1, input_grad(2, g_three, 15, start), norm_two[pl.ds(start, CH)],
            inv_two[pl.ds(start, CH)],
        )
        g_two[pl.ds(start, CH)] = value
        keep_masked(1, start, value)

    go(g_two.at[0:4], g_two.at[FR :], HALO_AT + 4, before_id)
    to_plane(0)
    weight_grad(1, ext_two, 12, g_two)
    to_sister(1)

    @pl.loop(0, FR // CH)
    def _(i):
        start = i * CH

        @pl.when(i == FR // CH - 1)
        def _():
            wait_for(g_two.at[FR :], HALO_AT + 4)

        value = norm_back(
            0, input_grad(1, g_two, 12, start), conv_one[pl.ds(start, CH)],
            inv_one[pl.ds(start, CH)],
        )
        g_one[pl.ds(start, CH)] = value
        for tap in (1, 2):
            kept = value.astype(F32) * mask[tap - 1, pl.ds(start, CH)]
            masked[tap - 1, pl.ds(start + 2 - tap, CH)] = kept.astype(BF16)

    remote(g_one.at[0:2], g_one.at[FR :], HALO_AT + 5, before_id).start()
    go(gain_sum, gain_sister, GAIN_AT, sister)
    to_row(0)
    to_plane(1)

    def first_weight_grad(tap):
        if tap == 0:
            right = g_one[0:FR]
        else:
            right = masked[tap - 1, 2 : FR + 2]
        right = right.reshape(FR * CELLS, C)
        for q in range(4):
            left = packed[:, :, q * C : (q + 1) * C].reshape(FR * CELLS, C)
            wacc[4 * tap + q] = lax.dot_general(
                left, right, (((0,), (0,)), ((), ())), preferred_element_type=F32
            )

    first_weight_grad(0)
    to_sister(2)
    wait_for(gain_sister, GAIN_AT)
    gain_plane[chip] = gain_sum[...] + gain_sister[...]
    for k in range(15):
        go(gain_plane.at[chip], gain_plane.at[chip], GAIN_AT + 1 + k, plane[k])
    to_owner(0)
    to_row(1)
    late_grad = g_one.at[FR :]
    remote(g_one.at[0:2], late_grad, HALO_AT + 5, before_id).wait()
    kept = late_grad[...].astype(F32)
    masked[0, FR + 1] = (kept[0] * mask[0, FR]).astype(BF16)
    masked[1, FR :] = (kept * mask[1, FR : FR + 2]).astype(BF16)
    first_weight_grad(1)
    to_sister(3)
    to_plane(2)
    for k, (dz, dy) in enumerate(ORDER):
        wait_for(gain_plane.at[(z - dz) % 4 * 4 + (y - dy) % 4], GAIN_AT + 1 + k)
    gain_all = gain_plane[0]
    for k in range(1, 16):
        gain_all = gain_all + gain_plane[k]
    gain_row[x] = gain_all
    for k in range(3):
        go(gain_row.at[x], gain_row.at[x], GAIN_AT + 16 + k, row[k])
    to_owner(1)
    first_weight_grad(2)
    to_sister(4)
    to_plane(3)
    to_row(2)
    to_plane(4)
    to_row(3)
    to_owner(2)
    to_row(4)
    to_owner(3)
    for k, d in enumerate((1, 2, 3)):
        wait_for(gain_row.at[(x - d) % 4], GAIN_AT + 16 + k)
    gain_out[...] = ((gain_row[0] + gain_row[1]) + gain_row[2]) + gain_row[3]
    to_owner(4)

    for g, (at, count) in enumerate(GROUPS):
        wait_for(last_in.at[pl.ds(at, count)], g * PER_GROUP + 19)
    for ref, at, count in ((out_one, 0, 12), (out_two, 12, 3), (out_three, 15, 3)):
        mine = total[at : at + count, our_rows, :]
        other = last_in[at : at + count]
        ref[:, :, :128] = jnp.where(low, mine, other)
        ref[:, :, 128:] = jnp.where(low, other, mine)
    remote(ext_two.at[FR :], ext_two.at[0:4], HALO_AT + 1, after_id).wait_send()
    remote(ext_three.at[FR :], ext_three.at[0:8], HALO_AT + 2, after_id).wait_send()
    for copy in started:
        copy.wait_send()


def shards(
    loaded, pack_dest, clip_lengths, weight_one, weight_two, weight_three, norm_gains, latent_grad
):
    block_index = lax.axis_index("dp") * 32 + lax.axis_index("chan")
    slots = jnp.arange(FR, dtype=jnp.int32)
    send_slot = pack_dest // FR % 32
    order = jnp.sum(jnp.where(send_slot[None, :] == slots[:, None], slots[None, :], 0), axis=1)
    own = jnp.concatenate(
        [weight_one, weight_two, weight_three, jnp.zeros((2, 8, C), BF16)], axis=0
    )
    frame_ids = block_index * FR + jnp.arange(FR + 8, dtype=jnp.int32)
    offset = clip_place(clip_lengths, frame_ids)
    lags = jnp.array([1, 2, 2, 4, 4, 8], jnp.int32)
    mask = jnp.broadcast_to(
        (offset[None, :] >= lags[:, None]).astype(F32)[:, :, None, None], (6, FR + 8, 1, C)
    )
    image = (CELLS, C)
    scratch = [
        ((2, C * FR, 128), F32),
        ((31, CELLS, 4 * C), BF16),
        ((FR, CELLS, 4 * C), BF16),
        ((20, C, C), BF16),
        ((20, 8, C), F32),
        ((20, 8, C), F32),
        ((20, 16, C), BF16),
        ((FR + 2,) + image, F32),
        ((2,) + image, F32),
        ((2,) + image, F32),
        ((FR + 4,) + image, BF16),
        ((FR + 8,) + image, BF16),
        ((FR,) + image, F32),
        ((FR, 1, C), F32),
        ((FR, 1, C), F32),
        ((FR + 2,) + image, BF16),
        ((FR + 4,) + image, BF16),
        ((FR + 8,) + image, BF16),
        ((2, FR + 2) + image, BF16),
        ((8, C), F32),
        ((18, C, C), F32),
        ((18, C, 128), BF16),
        ((18, C, 128), BF16),
        ((18, C, 128), BF16),
        ((15, 18, 16, 128), BF16),
        ((18, 16, 128), BF16),
        ((3, 18, 16, 128), BF16),
        ((18, 16, 128), F32),
        ((18, 8, 128), F32),
        ((8, C), F32),
        ((16, 8, C), F32),
        ((4, 8, C), F32),
    ]
    latent, out_one, out_two, out_three, gains = pl.pallas_call(
        kernel,
        out_shape=(
            jax.ShapeDtypeStruct((C, FR * CELLS), BF16),
            jax.ShapeDtypeStruct((12, 8, C), F32),
            jax.ShapeDtypeStruct((3, 8, C), F32),
            jax.ShapeDtypeStruct((3, 8, C), F32),
            jax.ShapeDtypeStruct((8, C), F32),
        ),
        in_specs=[SMEM_SPEC] + [VMEM_SPEC] * 5,
        out_specs=(VMEM_SPEC,) * 5,
        scratch_shapes=[pltpu.VMEM(shape, kind) for shape, kind in scratch]
        + [
            pltpu.SemaphoreType.DMA((N_SEM,)),
            pltpu.SemaphoreType.DMA((N_SEM,)),
            pltpu.SemaphoreType.DMA,
        ],
        compiler_params=pltpu.CompilerParams(
            collective_id=0, has_side_effects=True, vmem_limit_bytes=LIMIT
        ),
    )(order, loaded, own, mask, norm_gains, latent_grad)
    return (latent, out_one, out_two, out_three, gains[:3])


def solution(mesh):
    placed = (
        P(None, ("dp", "chan"), None),
        P(("dp", "chan")),
        P(),
        P(None, "chan", None),
        P(None, "chan", None),
        P(None, "chan", None),
        P(),
        P(None, ("dp", "chan")),
    )
    return jax.shard_map(
        shards,
        mesh=mesh,
        in_specs=placed,
        out_specs=(
            P(None, ("dp", "chan")),
            P(None, "chan", None),
            P(None, "chan", None),
            P(None, "chan", None),
            P(),
        ),
        check_vma=False,
    )
```

```python
import functools
import jax
import jax.numpy as jnp
from jax import lax
from jax.experimental import pallas as pl
from jax.experimental.pallas import tpu as pltpu
from jax.sharding import PartitionSpec as P

SIDE = 16
CELLS = 64
C = 256
FR = 32
EPS = 1e-05
DILATIONS = (1, 2, 4)
CH = 8
F32 = jnp.float32
BF16 = jnp.bfloat16
MESH = pl.DeviceIdType.MESH
VMEM_SPEC = pl.BlockSpec(memory_space=pltpu.VMEM)
ANY_SPEC = pl.BlockSpec(memory_space=pl.ANY)
LIMIT = 60 << 20


def sigmoid(value):
    return 0.5 * jnp.tanh(0.5 * value) + 0.5


ORDER = (
    (0, 1), (3, 0), (0, 3), (1, 0), (1, 1), (3, 3), (1, 3), (3, 1),
    (0, 2), (2, 0), (2, 2), (1, 2), (2, 3), (3, 2), (2, 1),
)
FRAME_OFFSETS = (
    tuple((dz, dy, 0) for dz, dy in ORDER)
    + ((0, 0, 1),)
    + tuple((dz, dy, 1) for dz, dy in ORDER)
    + ((0, 0, 0),)
)
GROUPS = ((15, 3), (12, 3), (0, 4), (4, 4), (8, 4))
NG = len(GROUPS)
PER_GROUP = 22
GAIN_AT = NG * PER_GROUP
HALO_AT = GAIN_AT + 19
WEIGHT_AT = HALO_AT + 6
FRAME_AT = WEIGHT_AT + 11
N_SEM = FRAME_AT + 62


def mean_of(value):
    part = jnp.sum(value.reshape(-1, 8, 8, C), axis=1)
    part = part[:, :, :128] + part[:, :, 128:]
    return jnp.sum(part, axis=(1, 2), keepdims=True) * (1.0 / (CELLS * C))


def kernel(
    dest_far, lengths_far, loaded_far, one_far, two_far, three_far, gains_far, cotangent_far,
    latent_far, out_one, out_two, out_three, gain_out,
    dest, lengths, weight_one, weight_two, weight_three, gains, order_near, order,
    loaded, cotangent, latent, mask,
    wide, send, packed, turned_one, full, own_f32, theirs_f32, wblk,
    conv_one, early_conv, late_conv, ext_two, turned_two, ext_three, turned_three, norm_two,
    inv_one, inv_two, g_one, g_two, g_three, masked, gain_part, gain_sum,
    wacc, sister_out, sister_in, chip_sum, plane_in, row_out, row_in, total, tap_out, tap_in, tap_sum, tap_plane, tap_total,
    gain_sister, gain_plane, gain_row, send_sem, recv_sem, local_sem,
):
    x, chan = lax.axis_index("dp"), lax.axis_index("chan")
    z, y, core = chan // 8, chan // 2 % 4, chan % 2
    chip = z * 4 + y
    low = core == 0

    def at_chan(zz, yy, cc):
        return zz * 8 + yy * 2 + cc

    index = x * 32 + chan
    after, before = (index + 1) % 128, (index + 127) % 128
    after_id = (after // 32, after % 32)
    before_id = (before // 32, before % 32)
    sister = (x, at_chan(z, y, 1 - core))
    plane = [(x, at_chan((z + dz) % 4, (y + dy) % 4, core)) for dz, dy in ORDER]
    row = [((x + d) % 4, chan) for d in (1, 2, 3)]
    partner = [
        at_chan((z + dz) % 4, (y + dy) % 4, (core + dc) % 2) for dz, dy, dc in FRAME_OFFSETS
    ]
    origin = [
        at_chan((z - dz) % 4, (y - dy) % 4, (core + dc) % 2) for dz, dy, dc in FRAME_OFFSETS
    ]

    barrier = pltpu.get_barrier_semaphore()
    for device in [(x, p) for p in partner[:31]] + row + [after_id, before_id]:
        pl.semaphore_signal(barrier, inc=1, device_id=device, device_id_type=MESH)

    loads = [
        pltpu.make_async_copy(
            loaded_far.at[pl.ds(32 * n, 32)], loaded.at[pl.ds(32 * n, 32)], local_sem.at[n]
        )
        for n in range(8)
    ]
    for copy in loads:
        copy.start()
    load_cotangent = pltpu.make_async_copy(cotangent_far, cotangent, local_sem.at[8])
    load_cotangent.start()
    small = [
        pltpu.make_async_copy(far, near, local_sem.at[11 + n])
        for n, (far, near) in enumerate((
            (dest_far, dest), (lengths_far, lengths), (one_far, weight_one),
            (two_far, weight_two), (three_far, weight_three), (gains_far, gains),
        ))
    ]
    for copy in small:
        copy.start()
    started = []

    def remote(src, dst, n, device):
        return pltpu.make_async_remote_copy(
            src_ref=src, dst_ref=dst, send_sem=send_sem.at[n], recv_sem=recv_sem.at[n],
            device_id=device, device_id_type=MESH,
        )

    def go(src, dst, n, device):
        copy = remote(src, dst, n, device)
        copy.start()
        started.append(copy)

    def wait_for(dst, n):
        remote(dst, dst, n, (x, chan)).wait_recv()

    small[0].wait()
    frames = lax.broadcasted_iota(jnp.int32, (FR, FR), 1)
    targets = lax.broadcasted_iota(jnp.int32, (FR, FR), 0)
    chosen = jnp.where(((dest[...] >> 5) & 31) == targets, frames, 0)
    order_near[...] = jnp.broadcast_to(jnp.max(chosen, axis=1, keepdims=True), (FR, 128))
    to_scalars = pltpu.make_async_copy(order_near, order, local_sem.at[17])
    to_scalars.start()
    for copy in small[1:]:
        copy.wait()
    own_f32[0:12] = weight_one[...].astype(F32)
    own_f32[12:15] = weight_two[...].astype(F32)
    own_f32[15:18] = weight_three[...].astype(F32)
    own_f32[18:] = jnp.zeros((2, 8, C), F32)
    cells_in = lax.broadcasted_iota(jnp.int32, (SIDE * SIDE, SIDE * SIDE), 1)
    cells_out = lax.broadcasted_iota(jnp.int32, (SIDE * SIDE, SIDE * SIDE), 0)
    in_row, in_col = cells_in // SIDE, cells_in % SIDE
    place = (2 * (in_row % 2) + in_col % 2) * CELLS + (in_row // 2) * (SIDE // 2) + in_col // 2
    pick = jnp.where(place == cells_out, 1.0, 0.0).astype(BF16)
    for part in range(8):
        loads[part].wait()
        for lane in range(2):
            block = loaded[part * 32 : part * 32 + 32, :, lane * 128 : lane * 128 + 128]
            wide[lane, part * 1024 : part * 1024 + 1024, :] = block.astype(F32).reshape(1024, 128)
    pl.semaphore_wait(barrier, 36)
    go(own_f32, theirs_f32, WEIGHT_AT, sister)

    to_scalars.wait()

    def image_of(target):
        frame = jnp.clip(order[target, 0], 0, FR - 1)
        halves = [
            wide.at[lane][pl.ds(frame, C, stride=FR), :].astype(BF16) for lane in range(2)
        ]
        cells = lax.dot_general(
            pick, jnp.concatenate(halves, axis=1), (((1,), (1,)), ((), ())),
            preferred_element_type=F32,
        ).astype(BF16)
        return jnp.concatenate(
            [cells[tap * CELLS : (tap + 1) * CELLS] for tap in range(4)], axis=1
        )

    def send_half(k, half):
        rows = pl.ds(half * 32, 32)
        go(
            send.at[k, rows], packed.at[chan, rows], FRAME_AT + 2 * k + half, (x, partner[k])
        )

    def send_frames(first, last):
        for k in range(first, last):
            send[k] = image_of(partner[k])
            send_half(k, 0)

    my_taps = pl.ds(5 * x, 5)
    my_rows = pl.ds(pl.multiple_of(chip * 16, 16), 16)
    my_plane = pl.ds(pl.multiple_of(z * 64, 64), 64)

    send_frames(0, 4)
    wait_for(theirs_f32, WEIGHT_AT)
    mine_w, their_w = own_f32[...], theirs_f32[...]
    both_w = jnp.concatenate(
        [jnp.where(low, mine_w, their_w), jnp.where(low, their_w, mine_w)], axis=1
    )
    wblk[...] = jnp.where(low, both_w[:, :, :128], both_w[:, :, 128:]).astype(BF16)
    local = pltpu.make_async_copy(
        wblk.at[my_taps], full.at[my_taps, core, my_rows], local_sem.at[9]
    )
    local.start()
    for d in (1, 2, 3):
        go(
            wblk.at[my_taps], full.at[my_taps, core, my_rows],
            WEIGHT_AT + d, (x, at_chan(z, (y + d) % 4, core)),
        )
    send_frames(4, 8)
    local.wait()
    for d in (1, 2, 3):
        rows = pl.ds(pl.multiple_of((z * 4 + (y - d) % 4) * 16, 16), 16)
        wait_for(full.at[my_taps, core, rows], WEIGHT_AT + d)
    block = full.at[my_taps, core, my_plane]
    for d in (1, 2, 3):
        go(block, block, WEIGHT_AT + 3 + d, (x, at_chan((z + d) % 4, y, core)))
    send_frames(8, 14)
    for d in (1, 2, 3):
        rows = pl.ds(pl.multiple_of((z - d) % 4 * 64, 64), 64)
        wait_for(full.at[my_taps, core, rows], WEIGHT_AT + 3 + d)
    block = full.at[my_taps, core]
    for d in (1, 2, 3):
        go(block, block, WEIGHT_AT + 6 + d, row[d - 1])
    send_frames(14, 31)
    for k in range(31):
        send_half(k, 1)
    packed[chan] = image_of(chan)

    lens = jnp.broadcast_to(lengths[...].astype(F32), (8, 512)).astype(BF16)
    earlier = lax.broadcasted_iota(jnp.int32, (512, 512), 0)
    later = lax.broadcasted_iota(jnp.int32, (512, 512), 1)
    before_it = jnp.where(earlier < later, 1.0, 0.0).astype(BF16)
    starts = jnp.dot(lens, before_it, preferred_element_type=F32)[0:1]
    frame = (lax.broadcasted_iota(jnp.int32, (FR + 8, 512), 0) + index * FR).astype(F32)
    start_of = jnp.max(jnp.where(starts <= frame, starts, -1.0), axis=1, keepdims=True)
    offset = jnp.where(frame[:, 0:1] < 4096.0, frame[:, 0:1] - start_of, 0.0)
    for n, lag in enumerate((1, 2, 2, 4, 4, 8)):
        kept = jnp.where(offset >= float(lag), 1.0, 0.0)
        mask[n] = jnp.broadcast_to(kept, (FR + 8, C)).reshape(FR + 8, 1, C)

    for d in (1, 2, 3):
        wait_for(full.at[pl.ds(5 * ((x - d) % 4), 5), core], WEIGHT_AT + 6 + d)
    block = full.at[:, core]
    go(block, block, WEIGHT_AT + 10, sister)
    wait_for(full.at[:, 1 - core], WEIGHT_AT + 10)

    def weights_of(first, count):
        halves = full[first : first + count]
        return jnp.concatenate([halves[:, 0], halves[:, 1]], axis=2).reshape(count * C, C)

    conv_one[...] = jnp.zeros_like(conv_one)

    def add_products(batch):
        slots = []
        for k in batch:
            if k < 31:
                for half in range(2):
                    rows = pl.ds(half * 32, 32)
                    wait_for(packed.at[origin[k], rows], FRAME_AT + 2 * k + half)
            slots.append(origin[k])
        rows = jnp.concatenate([packed[s] for s in slots], axis=0)
        for tap in range(3):
            term = jnp.dot(
                rows, weights_of(4 * tap, 4), preferred_element_type=F32
            )
            for n, s in enumerate(slots):
                piece = term[n * CELLS : (n + 1) * CELLS]
                if tap > 0:
                    piece = piece * mask[tap - 1, s + tap]
                conv_one[s + tap] += piece
        lanes = slice(batch[0] * CELLS, (batch[-1] + 1) * CELLS)
        for q in range(4):
            turned_one[q * C : (q + 1) * C, lanes] = rows[:, q * C : (q + 1) * C].T

    for first in range(0, 32, 8):
        add_products(range(first, first + 8))
    late_conv[...] = conv_one[FR:]
    go(late_conv, early_conv, HALO_AT, after_id)

    def gain_of(layer):
        return gains[layer : layer + 1, :].reshape(1, 1, C)

    def normalize(conv):
        mean = mean_of(conv)
        scale = lax.rsqrt(mean_of(conv * conv) - mean * mean + EPS)
        return (conv - mean) * scale, jnp.broadcast_to(scale, (conv.shape[0], 1, C))

    def conv_of(layer, src, first, start):
        step = DILATIONS[layer]
        conv = None
        for tap in range(3):
            rows = src[pl.ds(start + (2 - tap) * step, CH)].reshape(CH * CELLS, C)
            term = jnp.dot(rows, weights_of(first + tap, 1), preferred_element_type=F32)
            term = term.reshape(CH, CELLS, C)
            if tap == 0:
                conv = term
            else:
                conv = conv + term * mask[2 * layer + tap - 1, pl.ds(start, CH)]
        return conv

    def first_block(n):
        start = n * CH
        normed, scale = normalize(conv_one[pl.ds(start, CH)])
        conv_one[pl.ds(start, CH)] = normed
        inv_one[pl.ds(start, CH)] = scale
        scaled = gain_of(0) * normed
        act = (scaled * sigmoid(scaled)).reshape(CH * CELLS, C)
        ext_two[pl.ds(start + 4, CH)] = act.astype(BF16).reshape(CH, CELLS, C)
        turned_two[:, pl.ds((start + 4) * CELLS, CH * CELLS)] = act.T.astype(BF16)

    def second_block(n):
        start = n * CH
        normed, scale = normalize(conv_of(1, ext_two, 12, start))
        norm_two[pl.ds(start, CH)] = normed
        inv_two[pl.ds(start, CH)] = scale
        scaled = gain_of(1) * normed
        act = (scaled * sigmoid(scaled)).reshape(CH * CELLS, C)
        ext_three[pl.ds(start + 8, CH)] = act.astype(BF16).reshape(CH, CELLS, C)
        turned_three[:, pl.ds((start + 8) * CELLS, CH * CELLS)] = act.T.astype(BF16)

    def norm_back(layer, upstream, normed, scale):
        gain = gain_of(layer)
        scaled = gain * normed
        sig = sigmoid(scaled)
        scaled_grad = upstream * sig * (1.0 + scaled * (1.0 - sig))
        gain_part[layer] += jnp.sum((scaled_grad * normed).reshape(-1, 8, C), axis=0)
        normed_grad = scaled_grad * gain
        m1 = mean_of(normed_grad)
        m2 = mean_of(normed_grad * normed)
        return (scale * (normed_grad - m1 - normed * m2)).astype(BF16)

    def keep_masked(layer, start, value):
        for tap in (1, 2):
            kept = value.astype(F32) * mask[2 * layer + tap - 1, pl.ds(start, CH)]
            masked[tap - 1, pl.ds(start, CH)] = kept.astype(BF16)

    gain_part[...] = jnp.zeros_like(gain_part)
    load_cotangent.wait()

    def third_block(n):
        start = n * CH
        normed, scale = normalize(conv_of(2, ext_three, 15, start))
        scaled = gain_of(2) * normed
        act = scaled * sigmoid(scaled)
        lanes = pl.ds(start * CELLS, CH * CELLS)
        latent[:, lanes] = act.reshape(CH * CELLS, C).T.astype(BF16)
        upstream = cotangent[:, lanes].astype(F32).T.reshape(CH, CELLS, C)
        value = norm_back(2, upstream, normed, scale)
        g_three[pl.ds(start, CH)] = value
        keep_masked(2, start, value)

    first_block(3)
    go(ext_two.at[FR :], ext_two.at[0:4], HALO_AT + 1, after_id)
    first_block(2)
    second_block(3)
    go(ext_three.at[FR :], ext_three.at[0:8], HALO_AT + 2, after_id)
    first_block(1)
    second_block(2)
    third_block(3)
    wait_for(early_conv, HALO_AT)
    conv_one[0:2] += early_conv[...]
    first_block(0)
    second_block(1)
    third_block(2)
    wait_for(ext_two.at[0:4], HALO_AT + 1)
    turned_two[:, 0 : 4 * CELLS] = ext_two[0:4].reshape(4 * CELLS, C).T
    second_block(0)
    third_block(1)
    wait_for(ext_three.at[0:8], HALO_AT + 2)
    turned_three[:, 0 : 8 * CELLS] = ext_three[0:8].reshape(8 * CELLS, C).T
    third_block(0)
    go(g_three.at[0:8], g_three.at[FR :], HALO_AT + 3, before_id)
    store_latent = pltpu.make_async_copy(latent, latent_far, local_sem.at[10])
    store_latent.start()

    def weight_grad(layer, turned, at, grad):
        step = DILATIONS[layer]
        for tap in range(3):
            right = grad[0:FR] if tap == 0 else masked[tap - 1]
            lanes = slice((2 - tap) * step * CELLS, ((2 - tap) * step + FR) * CELLS)
            wacc[at + tap] = jnp.dot(
                turned[:, lanes], right.reshape(FR * CELLS, C), preferred_element_type=F32
            )

    def owned(k, first_core):
        value = wacc[k].reshape(16, 2, 8, C)
        value = jnp.where(first_core, value[:, 0], value[:, 1])
        return jnp.concatenate([value[:, :, :128], value[:, :, 128:]], axis=1).reshape(C, 128)

    def to_sister(g):
        at, count = GROUPS[g]
        for k in range(at, at + count):
            sister_out[k] = owned(k, core == 1).astype(BF16)
        taps = pl.ds(at, count)
        go(sister_out.at[taps], sister_in.at[taps], g * PER_GROUP, sister)

    def to_plane(g):
        at, count = GROUPS[g]
        taps = pl.ds(at, count)
        wait_for(sister_in.at[taps], g * PER_GROUP)
        for k in range(at, at + count):
            value = (owned(k, low) + sister_in[k].astype(F32)).astype(BF16)
            chip_sum[:, k] = value.reshape(16, 16, 128)
        for k, (dz, dy) in enumerate(ORDER):
            to = (z + dz) % 4 * 4 + (y + dy) % 4
            go(chip_sum.at[to, taps], plane_in.at[k, taps], g * PER_GROUP + 1 + k, plane[k])

    def to_row(g):
        at, count = GROUPS[g]
        taps = pl.ds(at, count)
        value = chip_sum[chip, taps].astype(F32)
        for k in range(15):
            wait_for(plane_in.at[k, taps], g * PER_GROUP + 1 + k)
            value = value + plane_in[k, taps].astype(F32)
        total[taps] = value
        row_out[taps] = value.astype(BF16)
        for k in range(3):
            go(row_out.at[taps], row_in.at[k, taps], g * PER_GROUP + 16 + k, row[k])

    def finish(g):
        at, count = GROUPS[g]
        taps = pl.ds(at, count)
        value = total[taps]
        for k in range(3):
            wait_for(row_in.at[k, taps], g * PER_GROUP + 16 + k)
            value = value + row_in[k, taps].astype(F32)
        value = jnp.concatenate([value[:, 0:8], value[:, 8:16]], axis=2)
        if at == 15:
            out_three[...] = value
        elif at == 12:
            out_two[...] = value
        else:
            out_one[taps] = value

    def row_first(g):
        at, count = GROUPS[g]
        taps = pl.ds(at, count)
        wait_for(sister_in.at[taps], g * PER_GROUP)
        for k in range(at, at + count):
            tap_out[k - at] = (owned(k, low) + sister_in[k].astype(F32)).astype(BF16)
        for k, d in enumerate((1, 2, 3)):
            go(tap_out.at[(x + d) % 4], tap_in.at[k], g * PER_GROUP + 16 + k, row[k])

    def plane_next(g):
        value = tap_out[x].astype(F32)
        for k in range(3):
            wait_for(tap_in.at[k], g * PER_GROUP + 16 + k)
            value = value + tap_in[k].astype(F32)
        tap_sum[...] = value.astype(BF16)
        for k, (dz, dy) in enumerate(ORDER):
            to = (z + dz) % 4 * 4 + (y + dy) % 4
            rows = pl.ds(pl.multiple_of(to * 16, 16), 16)
            go(tap_sum.at[rows, :], tap_plane.at[k], g * PER_GROUP + 1 + k, plane[k])

    def row_again(g):
        value = tap_sum[my_rows, :].astype(F32)
        for k in range(15):
            wait_for(tap_plane.at[k], g * PER_GROUP + 1 + k)
            value = value + tap_plane[k].astype(F32)
        tap_total[x] = value
        for k in range(3):
            go(tap_total.at[x], tap_total.at[x], g * PER_GROUP + 19 + k, row[k])

    def finish_row(g):
        at, count = GROUPS[g]
        for k, d in enumerate((1, 2, 3)):
            wait_for(tap_total.at[(x - d) % 4], g * PER_GROUP + 19 + k)
        value = tap_total[...]
        out_one[at : at + count] = jnp.concatenate([value[:, 0:8], value[:, 8:16]], axis=2)

    weight_grad(2, turned_three, 15, g_three)
    to_sister(0)

    def input_grad(layer, src, first, start):
        step = DILATIONS[layer]
        grad = None
        for tap in range(3):
            rows = src[pl.ds(start + tap * step, CH)].reshape(CH * CELLS, C)
            term = lax.dot_general(
                rows, weights_of(first + tap, 1), (((1,), (1,)), ((), ())), preferred_element_type=F32
            ).reshape(CH, CELLS, C)
            if tap == 0:
                grad = term
            else:
                grad = grad + term * mask[2 * layer + tap - 1, pl.ds(start + tap * step, CH)]
        return grad

    def second_back(n):
        start = n * CH
        value = norm_back(
            1, input_grad(2, g_three, 15, start), norm_two[pl.ds(start, CH)],
            inv_two[pl.ds(start, CH)],
        )
        g_two[pl.ds(start, CH)] = value
        keep_masked(1, start, value)

    def first_back(n):
        start = n * CH
        g_one[pl.ds(start, CH)] = norm_back(
            0, input_grad(1, g_two, 12, start), conv_one[pl.ds(start, CH)],
            inv_one[pl.ds(start, CH)],
        )

    second_back(0)
    go(g_two.at[0:4], g_two.at[FR :], HALO_AT + 4, before_id)
    second_back(1)
    to_plane(0)
    second_back(2)
    first_back(0)
    go(g_one.at[0:2], g_one.at[FR :], HALO_AT + 5, before_id)
    first_back(1)
    wait_for(g_three.at[FR :], HALO_AT + 3)
    second_back(3)
    weight_grad(1, turned_two, 12, g_two)
    to_sister(1)
    first_back(2)
    to_row(0)
    wait_for(g_two.at[FR :], HALO_AT + 4)
    first_back(3)
    gain_sum[...] = jnp.zeros_like(gain_sum)
    for n in range(3):
        gain_sum[n : n + 1, :] = jnp.sum(gain_part[n], axis=0, keepdims=True)
    go(gain_sum, gain_sister, GAIN_AT, sister)
    to_plane(1)

    def collect(tap):
        for k in range(32):
            value = g_one[origin[k] + tap]
            if tap > 0:
                value = (value.astype(F32) * mask[tap - 1, origin[k] + tap]).astype(BF16)
            masked[tap % 2, k] = value

    def first_weight_grad(tap):
        wacc[4 * tap : 4 * tap + 4] = jnp.dot(
            turned_one[...], masked[tap % 2].reshape(FR * CELLS, C), preferred_element_type=F32
        ).reshape(4, C, C)

    collect(0)
    first_weight_grad(0)
    to_sister(2)
    wait_for(gain_sister, GAIN_AT)
    gain_plane[chip] = gain_sum[...] + gain_sister[...]
    for k in range(15):
        go(gain_plane.at[chip], gain_plane.at[chip], GAIN_AT + 1 + k, plane[k])
    wait_for(g_one.at[FR :], HALO_AT + 5)
    collect(1)
    to_plane(2)
    first_weight_grad(1)
    to_sister(3)
    collect(2)
    row_first(3)
    first_weight_grad(2)
    to_sister(4)
    finish(0)
    to_row(1)
    to_plane(4)
    for k, (dz, dy) in enumerate(ORDER):
        wait_for(gain_plane.at[(z - dz) % 4 * 4 + (y - dy) % 4], GAIN_AT + 1 + k)
    gain_all = gain_plane[0]
    for k in range(1, 16):
        gain_all = gain_all + gain_plane[k]
    gain_row[x] = gain_all
    for k in range(3):
        go(gain_row.at[x], gain_row.at[x], GAIN_AT + 16 + k, row[k])
    plane_next(3)
    to_row(2)
    finish(1)
    row_again(3)
    to_row(4)
    finish(2)
    for k, d in enumerate((1, 2, 3)):
        wait_for(gain_row.at[(x - d) % 4], GAIN_AT + 16 + k)
    gain_out[...] = (((gain_row[0] + gain_row[1]) + gain_row[2]) + gain_row[3])[0:3]
    finish_row(3)
    finish(4)
    store_latent.wait()
    for copy in started:
        copy.wait_send()


def hand_on(*refs):
    far_in, far_out, near, sems = refs[:5], refs[5:10], refs[10:15], refs[15]
    arrive = [pltpu.make_async_copy(far_in[n], near[n], sems.at[n]) for n in range(5)]
    leave = [pltpu.make_async_copy(near[n], far_out[n], sems.at[n]) for n in range(5)]
    for copy in arrive:
        copy.start()
    for n in (1, 2, 3, 4, 0):
        arrive[n].wait()
        leave[n].start()
    for copy in leave:
        copy.wait()


def shards(
    loaded, pack_dest, clip_lengths, weight_one, weight_two, weight_three, norm_gains, latent_grad
):
    image = (CELLS, C)
    scratch = [
        ((1, FR), jnp.int32),
        ((1, 512), jnp.int32),
        ((12, 8, C), BF16),
        ((3, 8, C), BF16),
        ((3, 8, C), BF16),
        ((3, C), F32),
        ((FR, 128), jnp.int32),
        ((FR, 128), None),
        ((C, FR, SIDE * SIDE), BF16),
        ((C, FR * CELLS), BF16),
        ((C, FR * CELLS), BF16),
        ((6, FR + 8, 1, C), F32),
        ((2, C * FR, 128), F32),
        ((31, CELLS, 4 * C), BF16),
        ((FR, CELLS, 4 * C), BF16),
        ((4 * C, FR * CELLS), BF16),
        ((20, 2, C, 128), BF16),
        ((20, 8, C), F32),
        ((20, 8, C), F32),
        ((20, 16, 128), BF16),
        ((FR + 2,) + image, F32),
        ((2,) + image, F32),
        ((2,) + image, F32),
        ((FR + 4,) + image, BF16),
        ((C, (FR + 4) * CELLS), BF16),
        ((FR + 8,) + image, BF16),
        ((C, (FR + 8) * CELLS), BF16),
        ((FR,) + image, F32),
        ((FR, 1, C), F32),
        ((FR, 1, C), F32),
        ((FR + 2,) + image, BF16),
        ((FR + 4,) + image, BF16),
        ((FR + 8,) + image, BF16),
        ((2, FR) + image, BF16),
        ((3, 8, C), F32),
        ((8, C), F32),
        ((18, C, C), F32),
        ((18, C, 128), BF16),
        ((18, C, 128), BF16),
        ((16, 18, 16, 128), BF16),
        ((15, 18, 16, 128), BF16),
        ((18, 16, 128), BF16),
        ((3, 18, 16, 128), BF16),
        ((18, 16, 128), F32),
        ((4, C, 128), BF16),
        ((3, C, 128), BF16),
        ((C, 128), BF16),
        ((15, 16, 128), BF16),
        ((4, 16, 128), F32),
        ((8, C), F32),
        ((16, 8, C), F32),
        ((4, 8, C), F32),
    ]
    outs = pl.pallas_call(
        kernel,
        out_shape=(
            jax.ShapeDtypeStruct((C, FR * CELLS), BF16),
            jax.ShapeDtypeStruct((12, 8, C), F32),
            jax.ShapeDtypeStruct((3, 8, C), F32),
            jax.ShapeDtypeStruct((3, 8, C), F32),
            jax.ShapeDtypeStruct((3, C), F32),
        ),
        in_specs=[ANY_SPEC] * 8,
        out_specs=(ANY_SPEC,) + (VMEM_SPEC,) * 4,
        scratch_shapes=[
            pltpu.VMEM(shape, kind) if kind else pltpu.SMEM(shape, jnp.int32)
            for shape, kind in scratch
        ]
        + [
            pltpu.SemaphoreType.DMA((N_SEM,)),
            pltpu.SemaphoreType.DMA((N_SEM,)),
            pltpu.SemaphoreType.DMA((18,)),
        ],
        compiler_params=pltpu.CompilerParams(
            collective_id=0, has_side_effects=True, vmem_limit_bytes=LIMIT
        ),
    )(
        pack_dest.reshape(1, -1), clip_lengths.reshape(1, -1), loaded, weight_one, weight_two, weight_three,
        norm_gains, latent_grad,
    )
    return pl.pallas_call(
        hand_on,
        out_shape=tuple(jax.ShapeDtypeStruct(out.shape, out.dtype) for out in outs),
        in_specs=[ANY_SPEC] * 5,
        out_specs=(ANY_SPEC,) * 5,
        scratch_shapes=[pltpu.VMEM(out.shape, out.dtype) for out in outs]
        + [pltpu.SemaphoreType.DMA((5,))],
    )(*outs)


def solution(mesh):
    placed = (
        P(None, ("dp", "chan"), None),
        P(("dp", "chan")),
        P(),
        P(None, "chan", None),
        P(None, "chan", None),
        P(None, "chan", None),
        P(),
        P(None, ("dp", "chan")),
    )
    return jax.shard_map(
        shards,
        mesh=mesh,
        in_specs=placed,
        out_specs=(
            P(None, ("dp", "chan")),
            P(None, "chan", None),
            P(None, "chan", None),
            P(None, "chan", None),
            P(),
        ),
        check_vma=False,
    )
```

```python
import functools
import jax
import jax.numpy as jnp
from jax import lax
from jax.experimental import pallas as pl
from jax.experimental.pallas import tpu as pltpu
from jax.sharding import PartitionSpec as P

SIDE = 16
CELLS = 64
C = 256
FR = 32
EPS = 1e-05
DILATIONS = (1, 2, 4)
CH = 8
F32 = jnp.float32
BF16 = jnp.bfloat16
MESH = pl.DeviceIdType.MESH
VMEM_SPEC = pl.BlockSpec(memory_space=pltpu.VMEM)
ANY_SPEC = pl.BlockSpec(memory_space=pl.ANY)
LIMIT = 60 << 20


def sigmoid(value):
    return 0.5 * jnp.tanh(0.5 * value) + 0.5


ORDER = (
    (0, 1), (3, 0), (0, 3), (1, 0), (1, 1), (3, 3), (1, 3), (3, 1),
    (0, 2), (2, 0), (2, 2), (1, 2), (2, 3), (3, 2), (2, 1),
)
FRAME_OFFSETS = (
    tuple((dz, dy, 0) for dz, dy in ORDER)
    + ((0, 0, 1),)
    + tuple((dz, dy, 1) for dz, dy in ORDER)
    + ((0, 0, 0),)
)
GROUPS = ((15, 3), (12, 3), (0, 4), (4, 4), (8, 4))
NG = len(GROUPS)
PER_GROUP = 19
GAIN_AT = NG * PER_GROUP
HALO_AT = GAIN_AT + 19
WEIGHT_AT = HALO_AT + 6
FRAME_AT = WEIGHT_AT + 11
N_SEM = FRAME_AT + 62


def mean_of(value):
    part = jnp.sum(value.reshape(-1, 8, 8, C), axis=1)
    part = part[:, :, :128] + part[:, :, 128:]
    return jnp.sum(part, axis=(1, 2), keepdims=True) * (1.0 / (CELLS * C))


def kernel(
    dest_far, lengths_far, loaded_far, one_far, two_far, three_far, gains_far, cotangent_far,
    latent_far, out_one, out_two, out_three, gain_out,
    dest, lengths, weight_one, weight_two, weight_three, gains, order_near, order,
    loaded, cotangent, latent, mask,
    wide, send, packed, turned_one, full, own_f32, theirs_f32, wblk,
    conv_one, early_conv, late_conv, ext_two, turned_two, ext_three, turned_three, norm_two,
    inv_one, inv_two, g_one, g_two, g_three, masked, gain_part, gain_sum,
    wacc, sister_out, sister_in, chip_sum, plane_in, row_out, row_in, total,
    gain_sister, gain_plane, gain_row, send_sem, recv_sem, local_sem,
):
    x, chan = lax.axis_index("dp"), lax.axis_index("chan")
    z, y, core = chan // 8, chan // 2 % 4, chan % 2
    chip = z * 4 + y
    low = core == 0

    def at_chan(zz, yy, cc):
        return zz * 8 + yy * 2 + cc

    index = x * 32 + chan
    after, before = (index + 1) % 128, (index + 127) % 128
    after_id = (after // 32, after % 32)
    before_id = (before // 32, before % 32)
    sister = (x, at_chan(z, y, 1 - core))
    plane = [(x, at_chan((z + dz) % 4, (y + dy) % 4, core)) for dz, dy in ORDER]
    row = [((x + d) % 4, chan) for d in (1, 2, 3)]
    partner = [
        at_chan((z + dz) % 4, (y + dy) % 4, (core + dc) % 2) for dz, dy, dc in FRAME_OFFSETS
    ]
    origin = [
        at_chan((z - dz) % 4, (y - dy) % 4, (core + dc) % 2) for dz, dy, dc in FRAME_OFFSETS
    ]

    barrier = pltpu.get_barrier_semaphore()
    for device in [(x, p) for p in partner[:31]] + row + [after_id, before_id]:
        pl.semaphore_signal(barrier, inc=1, device_id=device, device_id_type=MESH)

    loads = [
        pltpu.make_async_copy(
            loaded_far.at[pl.ds(32 * n, 32)], loaded.at[pl.ds(32 * n, 32)], local_sem.at[n]
        )
        for n in range(8)
    ]
    for copy in loads:
        copy.start()
    load_cotangent = pltpu.make_async_copy(cotangent_far, cotangent, local_sem.at[8])
    load_cotangent.start()
    small = [
        pltpu.make_async_copy(far, near, local_sem.at[11 + n])
        for n, (far, near) in enumerate((
            (dest_far, dest), (lengths_far, lengths), (one_far, weight_one),
            (two_far, weight_two), (three_far, weight_three), (gains_far, gains),
        ))
    ]
    for copy in small:
        copy.start()
    started = []

    def remote(src, dst, n, device):
        return pltpu.make_async_remote_copy(
            src_ref=src, dst_ref=dst, send_sem=send_sem.at[n], recv_sem=recv_sem.at[n],
            device_id=device, device_id_type=MESH,
        )

    def go(src, dst, n, device):
        copy = remote(src, dst, n, device)
        copy.start()
        started.append(copy)

    def wait_for(dst, n):
        remote(dst, dst, n, (x, chan)).wait_recv()

    small[0].wait()
    frames = lax.broadcasted_iota(jnp.int32, (FR, FR), 1)
    targets = lax.broadcasted_iota(jnp.int32, (FR, FR), 0)
    chosen = jnp.where(((dest[...] >> 5) & 31) == targets, frames, 0)
    order_near[...] = jnp.broadcast_to(jnp.max(chosen, axis=1, keepdims=True), (FR, 128))
    to_scalars = pltpu.make_async_copy(order_near, order, local_sem.at[17])
    to_scalars.start()
    for copy in small[1:]:
        copy.wait()
    own_f32[0:12] = weight_one[...].astype(F32)
    own_f32[12:15] = weight_two[...].astype(F32)
    own_f32[15:18] = weight_three[...].astype(F32)
    own_f32[18:] = jnp.zeros((2, 8, C), F32)
    cells_in = lax.broadcasted_iota(jnp.int32, (SIDE * SIDE, SIDE * SIDE), 1)
    cells_out = lax.broadcasted_iota(jnp.int32, (SIDE * SIDE, SIDE * SIDE), 0)
    in_row, in_col = cells_in // SIDE, cells_in % SIDE
    place = (2 * (in_row % 2) + in_col % 2) * CELLS + (in_row // 2) * (SIDE // 2) + in_col // 2
    pick = jnp.where(place == cells_out, 1.0, 0.0).astype(BF16)
    for part in range(8):
        loads[part].wait()
        for lane in range(2):
            block = loaded[part * 32 : part * 32 + 32, :, lane * 128 : lane * 128 + 128]
            wide[lane, part * 1024 : part * 1024 + 1024, :] = block.astype(F32).reshape(1024, 128)
    pl.semaphore_wait(barrier, 36)
    go(own_f32, theirs_f32, WEIGHT_AT, sister)

    to_scalars.wait()

    def image_of(target):
        frame = jnp.clip(order[target, 0], 0, FR - 1)
        halves = [
            wide.at[lane][pl.ds(frame, C, stride=FR), :].astype(BF16) for lane in range(2)
        ]
        cells = lax.dot_general(
            pick, jnp.concatenate(halves, axis=1), (((1,), (1,)), ((), ())),
            preferred_element_type=F32,
        ).astype(BF16)
        return jnp.concatenate(
            [cells[tap * CELLS : (tap + 1) * CELLS] for tap in range(4)], axis=1
        )

    def send_half(k, half):
        rows = pl.ds(half * 32, 32)
        go(
            send.at[k, rows], packed.at[chan, rows], FRAME_AT + 2 * k + half, (x, partner[k])
        )

    def send_frames(first, last):
        for k in range(first, last):
            send[k] = image_of(partner[k])
            send_half(k, 0)

    my_taps = pl.ds(5 * x, 5)
    my_rows = pl.ds(pl.multiple_of(chip * 16, 16), 16)
    my_plane = pl.ds(pl.multiple_of(z * 64, 64), 64)

    send_frames(0, 4)
    wait_for(theirs_f32, WEIGHT_AT)
    mine_w, their_w = own_f32[...], theirs_f32[...]
    both_w = jnp.concatenate(
        [jnp.where(low, mine_w, their_w), jnp.where(low, their_w, mine_w)], axis=1
    )
    wblk[...] = jnp.where(low, both_w[:, :, :128], both_w[:, :, 128:]).astype(BF16)
    local = pltpu.make_async_copy(
        wblk.at[my_taps], full.at[my_taps, core, my_rows], local_sem.at[9]
    )
    local.start()
    for d in (1, 2, 3):
        go(
            wblk.at[my_taps], full.at[my_taps, core, my_rows],
            WEIGHT_AT + d, (x, at_chan(z, (y + d) % 4, core)),
        )
    send_frames(4, 8)
    local.wait()
    for d in (1, 2, 3):
        rows = pl.ds(pl.multiple_of((z * 4 + (y - d) % 4) * 16, 16), 16)
        wait_for(full.at[my_taps, core, rows], WEIGHT_AT + d)
    block = full.at[my_taps, core, my_plane]
    for d in (1, 2, 3):
        go(block, block, WEIGHT_AT + 3 + d, (x, at_chan((z + d) % 4, y, core)))
    send_frames(8, 14)
    for d in (1, 2, 3):
        rows = pl.ds(pl.multiple_of((z - d) % 4 * 64, 64), 64)
        wait_for(full.at[my_taps, core, rows], WEIGHT_AT + 3 + d)
    block = full.at[my_taps, core]
    for d in (1, 2, 3):
        go(block, block, WEIGHT_AT + 6 + d, row[d - 1])
    send_frames(14, 31)
    for k in range(31):
        send_half(k, 1)
    packed[chan] = image_of(chan)

    lens = jnp.broadcast_to(lengths[...].astype(F32), (8, 512)).astype(BF16)
    earlier = lax.broadcasted_iota(jnp.int32, (512, 512), 0)
    later = lax.broadcasted_iota(jnp.int32, (512, 512), 1)
    before_it = jnp.where(earlier < later, 1.0, 0.0).astype(BF16)
    starts = jnp.dot(lens, before_it, preferred_element_type=F32)[0:1]
    frame = (lax.broadcasted_iota(jnp.int32, (FR + 8, 512), 0) + index * FR).astype(F32)
    start_of = jnp.max(jnp.where(starts <= frame, starts, -1.0), axis=1, keepdims=True)
    offset = jnp.where(frame[:, 0:1] < 4096.0, frame[:, 0:1] - start_of, 0.0)
    for n, lag in enumerate((1, 2, 2, 4, 4, 8)):
        kept = jnp.where(offset >= float(lag), 1.0, 0.0)
        mask[n] = jnp.broadcast_to(kept, (FR + 8, C)).reshape(FR + 8, 1, C)

    for d in (1, 2, 3):
        wait_for(full.at[pl.ds(5 * ((x - d) % 4), 5), core], WEIGHT_AT + 6 + d)
    block = full.at[:, core]
    go(block, block, WEIGHT_AT + 10, sister)
    wait_for(full.at[:, 1 - core], WEIGHT_AT + 10)

    def weights_of(first, count):
        halves = full[first : first + count]
        return jnp.concatenate([halves[:, 0], halves[:, 1]], axis=2).reshape(count * C, C)

    conv_one[...] = jnp.zeros_like(conv_one)

    def add_products(batch):
        slots = []
        for k in batch:
            if k < 31:
                for half in range(2):
                    rows = pl.ds(half * 32, 32)
                    wait_for(packed.at[origin[k], rows], FRAME_AT + 2 * k + half)
            slots.append(origin[k])
        rows = jnp.concatenate([packed[s] for s in slots], axis=0)
        for tap in range(3):
            term = jnp.dot(
                rows, weights_of(4 * tap, 4), preferred_element_type=F32
            )
            for n, s in enumerate(slots):
                piece = term[n * CELLS : (n + 1) * CELLS]
                if tap > 0:
                    piece = piece * mask[tap - 1, s + tap]
                conv_one[s + tap] += piece
        lanes = slice(batch[0] * CELLS, (batch[-1] + 1) * CELLS)
        for q in range(4):
            turned_one[q * C : (q + 1) * C, lanes] = rows[:, q * C : (q + 1) * C].T

    for first in range(0, 32, 8):
        add_products(range(first, first + 8))
    late_conv[...] = conv_one[FR:]
    go(late_conv, early_conv, HALO_AT, after_id)

    def gain_of(layer):
        return gains[layer : layer + 1, :].reshape(1, 1, C)

    def normalize(conv):
        mean = mean_of(conv)
        scale = lax.rsqrt(mean_of(conv * conv) - mean * mean + EPS)
        return (conv - mean) * scale, jnp.broadcast_to(scale, (conv.shape[0], 1, C))

    def conv_of(layer, src, first, start):
        step = DILATIONS[layer]
        conv = None
        for tap in range(3):
            rows = src[pl.ds(start + (2 - tap) * step, CH)].reshape(CH * CELLS, C)
            term = jnp.dot(rows, weights_of(first + tap, 1), preferred_element_type=F32)
            term = term.reshape(CH, CELLS, C)
            if tap == 0:
                conv = term
            else:
                conv = conv + term * mask[2 * layer + tap - 1, pl.ds(start, CH)]
        return conv

    def first_block(n):
        start = n * CH
        normed, scale = normalize(conv_one[pl.ds(start, CH)])
        conv_one[pl.ds(start, CH)] = normed
        inv_one[pl.ds(start, CH)] = scale
        scaled = gain_of(0) * normed
        act = (scaled * sigmoid(scaled)).reshape(CH * CELLS, C)
        ext_two[pl.ds(start + 4, CH)] = act.astype(BF16).reshape(CH, CELLS, C)
        turned_two[:, pl.ds((start + 4) * CELLS, CH * CELLS)] = act.T.astype(BF16)

    def second_block(n):
        start = n * CH
        normed, scale = normalize(conv_of(1, ext_two, 12, start))
        norm_two[pl.ds(start, CH)] = normed
        inv_two[pl.ds(start, CH)] = scale
        scaled = gain_of(1) * normed
        act = (scaled * sigmoid(scaled)).reshape(CH * CELLS, C)
        ext_three[pl.ds(start + 8, CH)] = act.astype(BF16).reshape(CH, CELLS, C)
        turned_three[:, pl.ds((start + 8) * CELLS, CH * CELLS)] = act.T.astype(BF16)

    def norm_back(layer, upstream, normed, scale):
        gain = gain_of(layer)
        scaled = gain * normed
        sig = sigmoid(scaled)
        scaled_grad = upstream * sig * (1.0 + scaled * (1.0 - sig))
        gain_part[layer] += jnp.sum((scaled_grad * normed).reshape(-1, 8, C), axis=0)
        normed_grad = scaled_grad * gain
        m1 = mean_of(normed_grad)
        m2 = mean_of(normed_grad * normed)
        return (scale * (normed_grad - m1 - normed * m2)).astype(BF16)

    def keep_masked(layer, start, value):
        for tap in (1, 2):
            kept = value.astype(F32) * mask[2 * layer + tap - 1, pl.ds(start, CH)]
            masked[tap - 1, pl.ds(start, CH)] = kept.astype(BF16)

    gain_part[...] = jnp.zeros_like(gain_part)
    load_cotangent.wait()

    def third_block(n):
        start = n * CH
        normed, scale = normalize(conv_of(2, ext_three, 15, start))
        scaled = gain_of(2) * normed
        act = scaled * sigmoid(scaled)
        lanes = pl.ds(start * CELLS, CH * CELLS)
        latent[:, lanes] = act.reshape(CH * CELLS, C).T.astype(BF16)
        upstream = cotangent[:, lanes].astype(F32).T.reshape(CH, CELLS, C)
        value = norm_back(2, upstream, normed, scale)
        g_three[pl.ds(start, CH)] = value
        keep_masked(2, start, value)

    first_block(3)
    go(ext_two.at[FR :], ext_two.at[0:4], HALO_AT + 1, after_id)
    first_block(2)
    second_block(3)
    go(ext_three.at[FR :], ext_three.at[0:8], HALO_AT + 2, after_id)
    first_block(1)
    second_block(2)
    third_block(3)
    wait_for(early_conv, HALO_AT)
    conv_one[0:2] += early_conv[...]
    first_block(0)
    second_block(1)
    third_block(2)
    wait_for(ext_two.at[0:4], HALO_AT + 1)
    turned_two[:, 0 : 4 * CELLS] = ext_two[0:4].reshape(4 * CELLS, C).T
    second_block(0)
    third_block(1)
    wait_for(ext_three.at[0:8], HALO_AT + 2)
    turned_three[:, 0 : 8 * CELLS] = ext_three[0:8].reshape(8 * CELLS, C).T
    third_block(0)
    go(g_three.at[0:8], g_three.at[FR :], HALO_AT + 3, before_id)
    store_latent = pltpu.make_async_copy(latent, latent_far, local_sem.at[10])
    store_latent.start()

    def weight_grad(layer, turned, at, grad):
        step = DILATIONS[layer]
        for tap in range(3):
            right = grad[0:FR] if tap == 0 else masked[tap - 1]
            lanes = slice((2 - tap) * step * CELLS, ((2 - tap) * step + FR) * CELLS)
            wacc[at + tap] = jnp.dot(
                turned[:, lanes], right.reshape(FR * CELLS, C), preferred_element_type=F32
            )

    def owned(k, first_core):
        value = wacc[k].reshape(16, 2, 8, C)
        value = jnp.where(first_core, value[:, 0], value[:, 1])
        return jnp.concatenate([value[:, :, :128], value[:, :, 128:]], axis=1).reshape(C, 128)

    def to_sister(g):
        at, count = GROUPS[g]
        for k in range(at, at + count):
            sister_out[k] = owned(k, core == 1).astype(BF16)
        taps = pl.ds(at, count)
        go(sister_out.at[taps], sister_in.at[taps], g * PER_GROUP, sister)

    def to_plane(g):
        at, count = GROUPS[g]
        taps = pl.ds(at, count)
        wait_for(sister_in.at[taps], g * PER_GROUP)
        for k in range(at, at + count):
            value = (owned(k, low) + sister_in[k].astype(F32)).astype(BF16)
            chip_sum[:, k] = value.reshape(16, 16, 128)
        for k, (dz, dy) in enumerate(ORDER):
            to = (z + dz) % 4 * 4 + (y + dy) % 4
            go(chip_sum.at[to, taps], plane_in.at[k, taps], g * PER_GROUP + 1 + k, plane[k])

    def to_row(g):
        at, count = GROUPS[g]
        taps = pl.ds(at, count)
        value = chip_sum[chip, taps].astype(F32)
        for k in range(15):
            wait_for(plane_in.at[k, taps], g * PER_GROUP + 1 + k)
            value = value + plane_in[k, taps].astype(F32)
        total[taps] = value
        row_out[taps] = value.astype(BF16)
        for k in range(3):
            go(row_out.at[taps], row_in.at[k, taps], g * PER_GROUP + 16 + k, row[k])

    def finish(g):
        at, count = GROUPS[g]
        taps = pl.ds(at, count)
        value = total[taps]
        for k in range(3):
            wait_for(row_in.at[k, taps], g * PER_GROUP + 16 + k)
            value = value + row_in[k, taps].astype(F32)
        value = jnp.concatenate([value[:, 0:8], value[:, 8:16]], axis=2)
        if at == 15:
            out_three[...] = value
        elif at == 12:
            out_two[...] = value
        else:
            out_one[taps] = value

    weight_grad(2, turned_three, 15, g_three)
    to_sister(0)

    def input_grad(layer, src, first, start):
        step = DILATIONS[layer]
        grad = None
        for tap in range(3):
            rows = src[pl.ds(start + tap * step, CH)].reshape(CH * CELLS, C)
            term = lax.dot_general(
                rows, weights_of(first + tap, 1), (((1,), (1,)), ((), ())), preferred_element_type=F32
            ).reshape(CH, CELLS, C)
            if tap == 0:
                grad = term
            else:
                grad = grad + term * mask[2 * layer + tap - 1, pl.ds(start + tap * step, CH)]
        return grad

    def second_back(n):
        start = n * CH
        value = norm_back(
            1, input_grad(2, g_three, 15, start), norm_two[pl.ds(start, CH)],
            inv_two[pl.ds(start, CH)],
        )
        g_two[pl.ds(start, CH)] = value
        keep_masked(1, start, value)

    def first_back(n):
        start = n * CH
        g_one[pl.ds(start, CH)] = norm_back(
            0, input_grad(1, g_two, 12, start), conv_one[pl.ds(start, CH)],
            inv_one[pl.ds(start, CH)],
        )

    second_back(0)
    go(g_two.at[0:4], g_two.at[FR :], HALO_AT + 4, before_id)
    second_back(1)
    to_plane(0)
    second_back(2)
    first_back(0)
    go(g_one.at[0:2], g_one.at[FR :], HALO_AT + 5, before_id)
    first_back(1)
    wait_for(g_three.at[FR :], HALO_AT + 3)
    second_back(3)
    weight_grad(1, turned_two, 12, g_two)
    to_sister(1)
    first_back(2)
    to_row(0)
    wait_for(g_two.at[FR :], HALO_AT + 4)
    first_back(3)
    gain_sum[...] = jnp.zeros_like(gain_sum)
    for n in range(3):
        gain_sum[n : n + 1, :] = jnp.sum(gain_part[n], axis=0, keepdims=True)
    go(gain_sum, gain_sister, GAIN_AT, sister)
    to_plane(1)

    def collect(tap):
        for k in range(32):
            value = g_one[origin[k] + tap]
            if tap > 0:
                value = (value.astype(F32) * mask[tap - 1, origin[k] + tap]).astype(BF16)
            masked[tap % 2, k] = value

    def first_weight_grad(tap):
        wacc[4 * tap : 4 * tap + 4] = jnp.dot(
            turned_one[...], masked[tap % 2].reshape(FR * CELLS, C), preferred_element_type=F32
        ).reshape(4, C, C)

    collect(0)
    first_weight_grad(0)
    to_sister(2)
    wait_for(gain_sister, GAIN_AT)
    gain_plane[chip] = gain_sum[...] + gain_sister[...]
    for k in range(15):
        go(gain_plane.at[chip], gain_plane.at[chip], GAIN_AT + 1 + k, plane[k])
    wait_for(g_one.at[FR :], HALO_AT + 5)
    collect(1)
    to_plane(2)
    first_weight_grad(1)
    to_sister(3)
    collect(2)
    to_plane(3)
    first_weight_grad(2)
    to_sister(4)
    finish(0)
    to_row(1)
    to_plane(4)
    for k, (dz, dy) in enumerate(ORDER):
        wait_for(gain_plane.at[(z - dz) % 4 * 4 + (y - dy) % 4], GAIN_AT + 1 + k)
    gain_all = gain_plane[0]
    for k in range(1, 16):
        gain_all = gain_all + gain_plane[k]
    gain_row[x] = gain_all
    for k in range(3):
        go(gain_row.at[x], gain_row.at[x], GAIN_AT + 16 + k, row[k])
    to_row(2)
    finish(1)
    to_row(3)
    finish(2)
    to_row(4)
    for k, d in enumerate((1, 2, 3)):
        wait_for(gain_row.at[(x - d) % 4], GAIN_AT + 16 + k)
    gain_out[...] = (((gain_row[0] + gain_row[1]) + gain_row[2]) + gain_row[3])[0:3]
    finish(3)
    finish(4)
    store_latent.wait()
    for copy in started:
        copy.wait_send()


def hand_on(*refs):
    far_in, far_out, near, sems = refs[:5], refs[5:10], refs[10:15], refs[15]
    arrive = [pltpu.make_async_copy(far_in[n], near[n], sems.at[n]) for n in range(5)]
    leave = [pltpu.make_async_copy(near[n], far_out[n], sems.at[n]) for n in range(5)]
    for copy in arrive:
        copy.start()
    for n in (1, 2, 3, 4, 0):
        arrive[n].wait()
        leave[n].start()
    for copy in leave:
        copy.wait()


def shards(
    loaded, pack_dest, clip_lengths, weight_one, weight_two, weight_three, norm_gains, latent_grad
):
    image = (CELLS, C)
    scratch = [
        ((1, FR), jnp.int32),
        ((1, 512), jnp.int32),
        ((12, 8, C), BF16),
        ((3, 8, C), BF16),
        ((3, 8, C), BF16),
        ((3, C), F32),
        ((FR, 128), jnp.int32),
        ((FR, 128), None),
        ((C, FR, SIDE * SIDE), BF16),
        ((C, FR * CELLS), BF16),
        ((C, FR * CELLS), BF16),
        ((6, FR + 8, 1, C), F32),
        ((2, C * FR, 128), F32),
        ((31, CELLS, 4 * C), BF16),
        ((FR, CELLS, 4 * C), BF16),
        ((4 * C, FR * CELLS), BF16),
        ((20, 2, C, 128), BF16),
        ((20, 8, C), F32),
        ((20, 8, C), F32),
        ((20, 16, 128), BF16),
        ((FR + 2,) + image, F32),
        ((2,) + image, F32),
        ((2,) + image, F32),
        ((FR + 4,) + image, BF16),
        ((C, (FR + 4) * CELLS), BF16),
        ((FR + 8,) + image, BF16),
        ((C, (FR + 8) * CELLS), BF16),
        ((FR,) + image, F32),
        ((FR, 1, C), F32),
        ((FR, 1, C), F32),
        ((FR + 2,) + image, BF16),
        ((FR + 4,) + image, BF16),
        ((FR + 8,) + image, BF16),
        ((2, FR) + image, BF16),
        ((3, 8, C), F32),
        ((8, C), F32),
        ((18, C, C), F32),
        ((18, C, 128), BF16),
        ((18, C, 128), BF16),
        ((16, 18, 16, 128), BF16),
        ((15, 18, 16, 128), BF16),
        ((18, 16, 128), BF16),
        ((3, 18, 16, 128), BF16),
        ((18, 16, 128), F32),
        ((8, C), F32),
        ((16, 8, C), F32),
        ((4, 8, C), F32),
    ]
    outs = pl.pallas_call(
        kernel,
        out_shape=(
            jax.ShapeDtypeStruct((C, FR * CELLS), BF16),
            jax.ShapeDtypeStruct((12, 8, C), F32),
            jax.ShapeDtypeStruct((3, 8, C), F32),
            jax.ShapeDtypeStruct((3, 8, C), F32),
            jax.ShapeDtypeStruct((3, C), F32),
        ),
        in_specs=[ANY_SPEC] * 8,
        out_specs=(ANY_SPEC,) + (VMEM_SPEC,) * 4,
        scratch_shapes=[
            pltpu.VMEM(shape, kind) if kind else pltpu.SMEM(shape, jnp.int32)
            for shape, kind in scratch
        ]
        + [
            pltpu.SemaphoreType.DMA((N_SEM,)),
            pltpu.SemaphoreType.DMA((N_SEM,)),
            pltpu.SemaphoreType.DMA((18,)),
        ],
        compiler_params=pltpu.CompilerParams(
            collective_id=0, has_side_effects=True, vmem_limit_bytes=LIMIT
        ),
    )(
        pack_dest.reshape(1, -1), clip_lengths.reshape(1, -1), loaded, weight_one, weight_two, weight_three,
        norm_gains, latent_grad,
    )
    return pl.pallas_call(
        hand_on,
        out_shape=tuple(jax.ShapeDtypeStruct(out.shape, out.dtype) for out in outs),
        in_specs=[ANY_SPEC] * 5,
        out_specs=(ANY_SPEC,) * 5,
        scratch_shapes=[pltpu.VMEM(out.shape, out.dtype) for out in outs]
        + [pltpu.SemaphoreType.DMA((5,))],
    )(*outs)


def solution(mesh):
    placed = (
        P(None, ("dp", "chan"), None),
        P(("dp", "chan")),
        P(),
        P(None, "chan", None),
        P(None, "chan", None),
        P(None, "chan", None),
        P(),
        P(None, ("dp", "chan")),
    )
    return jax.shard_map(
        shards,
        mesh=mesh,
        in_specs=placed,
        out_specs=(
            P(None, ("dp", "chan")),
            P(None, "chan", None),
            P(None, "chan", None),
            P(None, "chan", None),
            P(),
        ),
        check_vma=False,
    )
```
